128 devices in a mesh: tm: 4 (over y_lo, core), space: 32 (over x, z, y_hi).
Axes of the slice: x: 4, y: 4 (y_hi: 2, y_lo: 2; y = y_hi * 2 + y_lo), z: 4, core: 2. Of those that a mesh axis runs over, the one named last changes fastest.
Arguments:
- hidden_state: bfloat16 [16, 32, 2, 8, 512], P('tm', 'space'), may hold values from -20 to 20
- norm1_gain: float32 [512], replicated, may hold values from 0.25 to 1.75
- norm1_bias: float32 [512], replicated, may hold values from -3 to 3
- qkv_weight: bfloat16 [512, 1536], replicated, may hold values from -8 to 8
- out_weight: bfloat16 [512, 512], replicated, may hold values from -0.25 to 0.25
- out_bias: float32 [512], replicated, may hold values from -3 to 3
- conv1_weight: bfloat16 [3, 3, 3, 512, 512], replicated, may hold values from -0.0546875 to 0.0546875
- conv1_bias: float32 [512], replicated, may hold values from -3 to 3
- norm2_gain: float32 [512], replicated, may hold values from 0.25 to 1.75
- norm2_bias: float32 [512], replicated, may hold values from -3 to 3
- conv2_weight: bfloat16 [3, 3, 3, 512, 256], replicated, may hold values from -0.0546875 to 0.0546875
- conv2_bias: float32 [256], replicated, may hold values from -3 to 3
Outputs:
- decoded: bfloat16 [16, 32, 8, 32, 256], P('tm', 'space')
The draws below stay inside these ranges and needn't reach their ends.
All inputs are finite; a program needn't handle non-finite values.
Results may differ from the reference program's by a relative error of at most 0.017.
Values may be sent and summed in bfloat16 or wider, within the bound.
A program may use at most 128 MiB of HBM per device.

```python
import jax
import jax.numpy as jnp
from jax import lax

C = 512
C2 = 256
GROUPS = 32
GRID_W = 4
TILE_H = 2
TILE_W = 8
FRAMES = 16
TILES = 32


def draw_hidden_state(key, part):
    key = jax.random.fold_in(key, 11)
    key_base, key_offset = jax.random.split(key, 2)
    shape = (FRAMES, TILES, TILE_H, TILE_W, C)
    ramp = jnp.arange(TILES, dtype=jnp.float32) / max(TILES - 1, 1)
    base = jnp.clip(jax.random.normal(key_base, shape, jnp.float32), -4.0, 4.0)
    scale = 1.0 + 2.0 * ramp
    offset = 0.5 * jnp.clip(jax.random.normal(key_offset, (C,), jnp.float32), -4.0, 4.0)
    return (base * scale[None, :, None, None, None] + offset).astype(jnp.bfloat16)


def draw_qkv_weight(key, part):
    key = jax.random.fold_in(key, 12)
    base = jnp.clip(jax.random.normal(key, (C, 3 * C), jnp.float32), -4.0, 4.0) * C ** (-0.5)
    return base.astype(jnp.bfloat16)


def normal_values(own_key, extent, scale, reach, held_as=jnp.bfloat16):
    drawn = scale * jax.random.normal(own_key, extent, jnp.float32)
    return jnp.clip(drawn, min=-reach, max=reach).astype(held_as)


def setup_inputs(seed: int = 0) -> dict:
    streams_of = jax.random.split(jax.random.key(seed), 13)
    hidden_state = draw_hidden_state(jax.random.fold_in(streams_of[12], 71), 0)
    norm1_gain = jnp.clip(1.0 + 0.15 * jax.random.normal(streams_of[1], (C,), jnp.float32), 0.25, 1.75)
    norm1_bias = normal_values(streams_of[2], (C,), 0.5, 3.0, jnp.float32)
    qkv_weight = draw_qkv_weight(jax.random.fold_in(streams_of[12], 71), 0)
    out_weight = normal_values(streams_of[4], (C, C), C ** -0.5, 0.25)
    out_bias = normal_values(streams_of[5], (C,), 0.5, 3.0, jnp.float32)
    conv1_weight = normal_values(streams_of[6], (3, 3, 3, C, C), (27 * C) ** -0.5, 0.0546875)
    conv1_bias = normal_values(streams_of[7], (C,), 0.5, 3.0, jnp.float32)
    norm2_gain = jnp.clip(1.0 + 0.15 * jax.random.normal(streams_of[8], (C,), jnp.float32), 0.25, 1.75)
    norm2_bias = normal_values(streams_of[9], (C,), 0.5, 3.0, jnp.float32)
    conv2_weight = normal_values(streams_of[10], (3, 3, 3, C, C2), (27 * C) ** -0.5, 0.0546875)
    conv2_bias = normal_values(streams_of[11], (C2,), 0.5, 3.0, jnp.float32)
    return dict(hidden_state=hidden_state, norm1_gain=norm1_gain, norm1_bias=norm1_bias, qkv_weight=qkv_weight, out_weight=out_weight, out_bias=out_bias, conv1_weight=conv1_weight, conv1_bias=conv1_bias, norm2_gain=norm2_gain, norm2_bias=norm2_bias, conv2_weight=conv2_weight, conv2_bias=conv2_bias)


def to_image(tiled):
    frames, tiles, tile_rows, tile_cols, chans = tiled.shape
    rows_of_tiles = tiles // GRID_W
    grid = tiled.reshape(frames, rows_of_tiles, GRID_W, tile_rows, tile_cols, chans)
    return grid.transpose(0, 1, 3, 2, 4, 5).reshape(frames, rows_of_tiles * tile_rows, GRID_W * tile_cols, chans)

def to_tiles(image, tile_rows, tile_cols):
    frames, height, width, chans = image.shape
    rows_of_tiles = height // tile_rows
    grid = image.reshape(frames, rows_of_tiles, tile_rows, GRID_W, tile_cols, chans)
    return grid.transpose(0, 1, 3, 2, 4, 5).reshape(frames, rows_of_tiles * GRID_W, tile_rows, tile_cols, chans)

def group_norm(field, gain, bias):
    frames, height, width, chans = field.shape
    grouped = field.astype(jnp.float32).reshape(frames, height, width, GROUPS, chans // GROUPS)
    count = height * width * (chans // GROUPS)
    first_sum = lax.optimization_barrier(jnp.sum(grouped, axis=(1, 2, 4)))
    second_sum = lax.optimization_barrier(jnp.sum(grouped * grouped, axis=(1, 2, 4)))
    mean_val = first_sum / count
    var_val = second_sum / count - mean_val * mean_val
    scaled = (grouped - mean_val[:, None, None, :, None]) * lax.rsqrt(var_val + 1e-06)[:, None, None, :, None]
    return scaled.reshape(frames, height, width, chans) * gain + bias

def causal_conv(field, weight, bias):
    frames, height, width, chans = field.shape
    outs = weight.shape[-1]
    upsampled = jnp.repeat(jnp.repeat(field, 2, axis=1), 2, axis=2)
    padded = jnp.pad(upsampled, ((0, 0), (1, 1), (1, 1), (0, 0)))
    padded = jnp.concatenate([padded[:1], padded[:1], padded], axis=0)

    def one_frame(frame_idx):
        total = jnp.zeros((2 * height * 2 * width, outs), jnp.float32)
        for time_offset in range(3):
            plane = lax.dynamic_slice_in_dim(padded, frame_idx + time_offset, 1, 0)[0]
            for row_offset in range(3):
                pieces = [plane[row_offset:row_offset + 2 * height, column_offset:column_offset + 2 * width] for column_offset in range(3)]
                slab = jnp.concatenate(pieces, axis=-1).reshape(-1, 3 * chans)
                total = total + jnp.dot(slab, weight[time_offset, row_offset].reshape(3 * chans, outs), preferred_element_type=jnp.float32)
        return total.reshape(2 * height, 2 * width, outs)
    return lax.map(one_frame, jnp.arange(frames, dtype=jnp.int32)) + bias

def reference(hidden_state, norm1_gain, norm1_bias, qkv_weight, out_weight, out_bias, conv1_weight, conv1_bias, norm2_gain, norm2_bias, conv2_weight, conv2_bias):
    image = to_image(hidden_state)
    frames, height, width, chans = image.shape
    normed = group_norm(image, norm1_gain, norm1_bias).astype(jnp.bfloat16)
    projected = jnp.dot(normed.reshape(-1, chans), qkv_weight, preferred_element_type=jnp.float32)
    queries = projected[:, :chans].astype(jnp.bfloat16).reshape(frames, height * width, chans)
    keys = projected[:, chans:2 * chans].astype(jnp.bfloat16).reshape(frames, height * width, chans)
    values = projected[:, 2 * chans:].astype(jnp.bfloat16).reshape(frames, height * width, chans)
    scores = jnp.einsum('fpc,gpc->pfg', queries.astype(jnp.float32), keys.astype(jnp.float32)) * chans ** (-0.5)
    positions = jnp.arange(frames, dtype=jnp.int32)
    allowed = positions[None, None, :] <= positions[None, :, None]
    row_max = lax.optimization_barrier(jnp.max(jnp.where(allowed, scores, -1e+30), axis=-1))
    weights = jnp.where(allowed, jnp.exp(scores - row_max[..., None]), 0.0)
    row_total = lax.optimization_barrier(jnp.sum(weights, axis=-1))
    summed = jnp.einsum('pfg,gpc->fpc', weights.astype(jnp.bfloat16).astype(jnp.float32), values.astype(jnp.float32))
    attended = (summed / jnp.transpose(row_total)[..., None]).astype(jnp.bfloat16)
    output_proj = jnp.dot(attended.reshape(-1, chans), out_weight, preferred_element_type=jnp.float32) + out_bias
    mixed = (image.astype(jnp.float32) + output_proj.reshape(image.shape)).astype(jnp.bfloat16)
    first_section = causal_conv(mixed, conv1_weight, conv1_bias).astype(jnp.bfloat16)
    activated = jax.nn.silu(group_norm(first_section, norm2_gain, norm2_bias)).astype(jnp.bfloat16)
    decoded = causal_conv(activated, conv2_weight, conv2_bias).astype(jnp.bfloat16)
    return to_tiles(decoded, 4 * hidden_state.shape[2], 4 * hidden_state.shape[3])
```

```python
import jax
import jax.numpy as jnp
from jax import lax
from jax.experimental import pallas as pl
from jax.experimental.pallas import tpu as pltpu
from jax.sharding import PartitionSpec as P

F32, BF16 = jnp.float32, jnp.bfloat16
MESH = pl.DeviceIdType.MESH
C, C2, LANES = 512, 256, 128
CHUNKS = C // LANES
GRID_COLS, GRID_ROWS, TILES, SHARDS = 4, 8, 32, 4
FRAMES = 4
CELLS = 40
FAR = 21
EPS = 1e-6
RING = ((-1, 0), (1, 0), (0, -1), (0, 1), (-1, -1), (-1, 1), (1, -1), (1, 1))
RING_ROWS = (32, 32, 16, 16, 16, 16, 16, 16)
RING_AT = (64, 96, 128, 144, 160, 176, 192, 208)
BLOCK_ROWS = 224


def iota(shape, axis):
    return lax.broadcasted_iota(jnp.int32, shape, axis)


def lane_roll(value, shift):
    return pltpu.roll(value, shift % LANES, axis=value.ndim - 1)


def sub_roll(value, shift):
    return pltpu.roll(value, shift % 8, axis=value.ndim - 2)


def pack_sums(total, first_row):
    lane = iota((8, LANES), 1)
    row = iota((8, LANES), 0)
    merged = jnp.zeros((8, LANES), F32)
    for k in range(CHUNKS):
        part = total[:, k * LANES : (k + 1) * LANES]
        for step in (1, 2, 4, 8):
            part = part + lane_roll(part, -step)
        part = jnp.where((lane & 15) == 0, part, 0.0)
        merged = merged + (lane_roll(part, k) if k else part)
    placed = jnp.zeros((8, LANES), F32)
    for f in range(FRAMES):
        placed = placed + jnp.where(row == first_row + f, lane_roll(merged, 4 * f) if f else merged, 0.0)
    return jnp.sum(placed, axis=0, keepdims=True)


def group_stats(block, count):
    total = jnp.sum(block.reshape(8, 8, LANES), axis=0)
    total = total + sub_roll(total, 2)
    total = total + sub_roll(total, 4)
    mean = total[0:1] * (1.0 / count)
    square = total[1:2] * (1.0 / count)
    scale = lax.rsqrt(square - mean * mean + EPS)
    return jnp.broadcast_to(mean, (8, LANES)), jnp.broadcast_to(scale, (8, LANES))


def by_frame(first, second, second_rows, frames):
    row = iota((8, LANES), 0)
    out = jnp.zeros((8, LANES), F32)
    for f in range(FRAMES):
        moved = (lane_roll(first, -4 * f), lane_roll(second, -4 * f)) if f else (first, second)
        for r in range(8):
            if frames[r] == f:
                out = jnp.where(row == r, moved[1] if second_rows[r] else moved[0], out)
    return out


def spread(rows):
    lane = iota((8, LANES), 1)
    parts = []
    for k in range(CHUNKS):
        part = jnp.where((lane & 15) == 0, lane_roll(rows, -k) if k else rows, 0.0)
        for step in (1, 2, 4, 8):
            part = part + lane_roll(part, step)
        parts.append(part)
    return jnp.concatenate(parts, axis=1)


def kernel(
    hid_hbm, gain1_hbm, bias1_hbm, wqkv_hbm, wout_hbm, bout_hbm, w1_hbm, b1_hbm, gain2_hbm, bias2_hbm, w2_hbm, b2_hbm,
    out_ref,
    hid, gain1, bias1, wqkv, wout, bout, w1, b1, gain2, bias2, w2, b2,
    own, side, hbuf, sums, got1, got2, xhi, normed, queries, keys, values, attended, mixcat, t1, fs, actcat, t2,
    small_sem, w1_sem, w2_sem, hid_send, hid_recv, sum_send, sum_recv,
):
    tm = lax.axis_index("tm")
    sp = lax.axis_index("space")
    tile_row, tile_col = sp >> 2, sp & 3

    smalls = [
        pltpu.make_async_copy(a, b, small_sem.at[i])
        for i, (a, b) in enumerate(
            (
                (hid_hbm, hid), (wqkv_hbm, wqkv), (wout_hbm, wout), (gain1_hbm, gain1), (bias1_hbm, bias1),
                (bout_hbm, bout), (b1_hbm, b1), (gain2_hbm, gain2), (bias2_hbm, bias2), (b2_hbm, b2),
            )
        )
    ]
    for copy in smalls:
        copy.start()

    barrier = pltpu.get_barrier_semaphore()
    for kt in range(SHARDS):
        def greet(i, carry, kt=kt):
            ks = i ^ FAR

            def signal():
                pl.semaphore_signal(barrier, inc=1, device_id=(tm ^ kt, sp ^ ks), device_id_type=MESH)

            if kt:
                signal()
            else:
                pl.when(ks != 0)(signal)
            return carry

        lax.fori_loop(0, TILES, greet, 0)

    def tap_copies(i):
        a, be = i // 9, lax.rem(i, 9)
        rows = pl.ds(pl.multiple_of(a * C, C), C)
        return (
            pltpu.make_async_copy(w1_hbm.at[i], w1.at[be, rows], w1_sem.at[i]),
            pltpu.make_async_copy(w2_hbm.at[i], w2.at[be, rows], w2_sem.at[i]),
        )

    def start_first(i, carry):
        tap_copies(i)[0].start()
        return carry

    def start_second(i, carry):
        tap_copies(i)[1].start()
        return carry

    lax.fori_loop(0, 27, start_first, 0)
    lax.fori_loop(0, 27, start_second, 0)

    for dt in range(1, SHARDS):
        @pl.when(tm < dt)
        def _():
            hbuf[3 - dt] = jnp.zeros((BLOCK_ROWS, C), BF16)

    for copy in smalls:
        copy.wait()
    order_out, order_in = iota((64, 64), 0), iota((64, 64), 1)
    wanted = (order_out & 3) * 16 + (order_out >> 2)
    permute = jnp.where(order_in == wanted, 1.0, 0.0).astype(BF16)
    plain = hid[...].astype(F32).reshape(64, C).astype(BF16)
    mine = jnp.dot(permute, plain, preferred_element_type=F32)
    mine16 = mine.astype(BF16)
    own[...] = mine16
    hbuf[3, 0:64] = mine16
    side[0] = jnp.concatenate([mine[0:8], mine[32:40]], axis=0).astype(BF16)
    side[1] = jnp.concatenate([mine[24:32], mine[56:64]], axis=0).astype(BF16)
    pairs = mine.reshape(8, 8, C)
    first = jnp.sum(pairs, axis=0)
    second = jnp.sum(pairs * pairs, axis=0)
    first = first + sub_roll(first, 4)
    second = second + sub_roll(second, 4)
    packed = jnp.concatenate([pack_sums(first, 0), pack_sums(second, 0)], axis=0)
    sums[0] = packed
    got1[0:2] = packed

    pl.semaphore_wait(barrier, SHARDS * TILES - 1)

    def send_sums(which, target, slot, buf):
        pltpu.make_async_remote_copy(
            src_ref=sums.at[which], dst_ref=buf.at[pl.ds(pl.multiple_of(slot * 2, 2), 2)],
            send_sem=sum_send.at[which], recv_sem=sum_recv.at[which], device_id=target, device_id_type=MESH,
        ).start()

    for kt in range(SHARDS):
        def send_one(i, carry, kt=kt):
            ks = i ^ FAR

            def go():
                send_sums(0, (tm ^ kt, sp ^ ks), kt * TILES + ks, got1)

            if kt:
                go()
            else:
                pl.when(ks != 0)(go)
            return carry

        lax.fori_loop(0, TILES, send_one, 0)

    def piece(dr, dc):
        if dc == 0:
            return own.at[pl.ds(0, 32)] if dr < 0 else own.at[pl.ds(32, 32)]
        return side.at[0] if dc < 0 else side.at[1]

    for dt in (3, 2, 1, 0):
        @pl.when(tm + dt < SHARDS)
        def _(dt=dt):
            def push(src, at, rows, target):
                pltpu.make_async_remote_copy(
                    src_ref=src, dst_ref=hbuf.at[3 - dt, pl.ds(at, rows)], send_sem=hid_send.at[dt],
                    recv_sem=hid_recv.at[dt], device_id=target, device_id_type=MESH,
                ).start()

            for i in (4, 5, 6, 7, 0, 1, 2, 3):
                dr, dc = RING[i]
                there = ((tile_row + dr) & 7) * GRID_COLS + ((tile_col + dc) & 3)
                at = RING_AT[RING.index((-dr, -dc))]
                push(piece(dr, dc), at, RING_ROWS[i], (tm + dt, there))
            if dt:
                push(own, 0, 64, (tm + dt, sp))

    def block_copy(dt):
        ref = hbuf.at[3 - dt, pl.ds(64, 160)] if dt == 0 else hbuf.at[3 - dt]
        return pltpu.make_async_remote_copy(
            src_ref=ref, dst_ref=ref, send_sem=hid_send.at[dt], recv_sem=hid_recv.at[dt],
            device_id=(tm ^ 1, sp), device_id_type=MESH,
        )

    def sums_copy(which, buf, rows):
        ref = buf.at[pl.ds(2, rows - 2)]
        return pltpu.make_async_remote_copy(
            src_ref=ref, dst_ref=ref, send_sem=sum_send.at[which], recv_sem=sum_recv.at[which],
            device_id=(tm ^ 1, sp), device_id_type=MESH,
        )

    for dt in range(SHARDS):
        @pl.when(tm >= dt)
        def _(dt=dt):
            block_copy(dt).wait_recv()

    sums_copy(0, got1, 256).wait_recv()

    starting = tm == 0
    row8 = iota((8, LANES), 0)
    stats = []
    for dt in range(SHARDS):
        kt = tm ^ ((tm - dt) & 3)
        stats.append(group_stats(got1[pl.ds(pl.multiple_of(kt * 64, 64), 64)], TILES * 16 * 16))
    span = (0, 0, 0, 0, 1, 1, 1, 1)
    steps = (0, 1, 2, 3, 0, 1, 2, 3)
    normers = []
    for half in range(2):
        pair = []
        for which in range(2):
            rows = by_frame(stats[3 - 2 * half][which], stats[2 - 2 * half][which], span, steps)
            if half:
                rows = jnp.where(starting & (row8 < 4), jnp.broadcast_to(rows[4:5], (8, LANES)), rows)
            pair.append(spread(rows))
        normers.append((pair[0], pair[1] * gain1[...]))
    shift1 = bias1[...]
    low = iota((1, 8, C), 1) < 4

    def place(cells, parts, odd):
        halves = []
        for half in range(2):
            a, b = parts[2 * half], parts[2 * half + 1]
            if odd:
                a = sub_roll(a, 4)
            else:
                b = sub_roll(b, 4)
            halves.append(jnp.where(low, a, b))
        lo, hi = halves
        hi = jnp.where(starting & low, jnp.broadcast_to(hi[:, 4:5], hi.shape), hi)
        nlo = (lo - normers[0][0]) * normers[0][1] + shift1
        nhi = (hi - normers[1][0]) * normers[1][1] + shift1
        for i, cell in enumerate(cells):
            xhi[cell] = hi[i]
            normed[cell] = jnp.concatenate([nlo[i], nhi[i]], axis=0).astype(BF16)

    def rows_of(at, count):
        return [hbuf[s, at : at + count].astype(F32).reshape(count // 8, 8, C) for s in range(4)]

    for r in range(4):
        at = (64, 0, 32, 96)[r]
        parts = rows_of(at, 32)
        for odd in range(2):
            place([r * 10 + 1 + 2 * i + odd for i in range(4)], parts, odd)
    for i, cells in (
        (2, ((10, 0, 1), (20, 1, 1))), (3, ((19, 0, 0), (29, 1, 0))),
        (4, ((0, 1, 1),)), (5, ((9, 1, 0),)), (6, ((30, 0, 1),)), (7, ((39, 0, 0),)),
    ):
        parts = rows_of(RING_AT[i], 16)
        for cell, pair, odd in cells:
            place([cell], [p[pair : pair + 1] for p in parts], odd)

    for g in range(20):
        two = normed[2 * g : 2 * g + 2].astype(F32)
        queries[16 * g : 16 * g + 16] = jnp.concatenate([two[0, 8:16], two[1, 8:16]], axis=0).astype(BF16)
    asked = jnp.dot(queries[...], wqkv[:, 0:C], preferred_element_type=F32)
    queries[...] = asked.astype(BF16)
    everything = normed[...].reshape(CELLS * 16, C)
    keys[...] = jnp.dot(everything, wqkv[:, C : 2 * C], preferred_element_type=F32).astype(BF16)
    values[...] = jnp.dot(everything, wqkv[:, 2 * C :], preferred_element_type=F32).astype(BF16)

    q_row, k_col = iota((64, 128), 0), iota((64, 128), 1)
    first_frame = 12 - 4 * tm
    q_frame = jnp.maximum((q_row & 7) + 8, first_frame)
    k_frame = k_col & 15
    allowed = ((q_row >> 3) == (k_col >> 4)) & (k_frame <= q_frame) & (k_frame >= first_frame)
    for g in range(5):
        q = queries[64 * g : 64 * g + 64]
        k = keys[128 * g : 128 * g + 128]
        v = values[128 * g : 128 * g + 128]
        scores = lax.dot_general(q, k, (((1,), (1,)), ((), ())), preferred_element_type=F32) * C ** (-0.5)
        scores = jnp.where(allowed, scores, -1e30)
        weights = jnp.exp(scores - jnp.max(scores, axis=1, keepdims=True))
        weights = jnp.where(allowed, weights, 0.0)
        total = jnp.sum(weights, axis=1, keepdims=True)
        summed = jnp.dot(weights.astype(BF16), v, preferred_element_type=F32)
        attended[64 * g : 64 * g + 64] = (summed / total).astype(BF16)

    projected = jnp.dot(attended[...], wout[...], preferred_element_type=F32).reshape(CELLS, 8, C)
    top, bottom = tile_row == 0, tile_row == GRID_ROWS - 1
    leftmost, rightmost = tile_col == 0, tile_col == GRID_COLS - 1
    for r in range(4):
        mixed = (xhi[10 * r : 10 * r + 10] + (projected[10 * r : 10 * r + 10] + bout[...])).astype(BF16).astype(F32)
        col = iota((10, 8, C), 0)
        outside = (leftmost & (col == 0)) | (rightmost & (col == 9))
        if r == 0:
            outside = outside | top
        if r == 3:
            outside = outside | bottom
        mixed = jnp.where(outside, 0.0, mixed)
        for a in range(3):
            moved = sub_roll(mixed, -a) if a else mixed
            mixcat[80 * r : 80 * r + 80, a * C : (a + 1) * C] = moved.reshape(80, C).astype(BF16)

    def wait_first(i, carry):
        tap_copies(i)[0].wait()
        return carry

    lax.fori_loop(0, 27, wait_first, 0)

    def first_taps(e, carry):
        for b in range(3):
            begin, end = ((0, 240), (0, 320), (80, 320))[b]
            t1[b, e, begin:end] = jnp.dot(mixcat[begin:end], w1[3 * b + e], preferred_element_type=F32)
        return carry

    lax.fori_loop(0, 3, first_taps, 0)

    def t1_row(b, e, r, lanes):
        return t1[b, e, 80 * r : 80 * r + 80, lanes].reshape(10, 8, LANES)

    sum_first, sum_second = [], []
    for k in range(CHUNKS):
        lanes = slice(k * LANES, (k + 1) * LANES)
        acc, acc2 = jnp.zeros((8, LANES), F32), jnp.zeros((8, LANES), F32)
        for R in range(6):
            s = []
            for e in range(3):
                if R % 2 == 0:
                    r = R // 2
                    s.append(t1_row(0, e, r, lanes) + t1_row(1, e, r, lanes) + t1_row(2, e, r + 1, lanes))
                else:
                    r = (R + 1) // 2
                    s.append(t1_row(0, e, r - 1, lanes) + t1_row(1, e, r, lanes) + t1_row(2, e, r, lanes))
            even = s[0][0:9] + s[1][0:9] + s[2][1:10] + b1[:, lanes]
            odd = s[0][0:9] + s[1][1:10] + s[2][1:10] + b1[:, lanes]
            even = even.astype(BF16).astype(F32)
            odd = odd.astype(BF16).astype(F32)
            fs[R, 0, :, :, lanes] = even
            fs[R, 1, :, :, lanes] = odd
            if 1 <= R <= 4:
                inner_e, inner_o = even[1:9], odd[0:8]
                acc = acc + jnp.sum(inner_e, axis=0) + jnp.sum(inner_o, axis=0)
                acc2 = acc2 + jnp.sum(inner_e * inner_e, axis=0) + jnp.sum(inner_o * inner_o, axis=0)
        sum_first.append(acc)
        sum_second.append(acc2)
    packed = jnp.concatenate(
        [pack_sums(jnp.concatenate(sum_first, axis=1), 2), pack_sums(jnp.concatenate(sum_second, axis=1), 2)], axis=0
    )
    sums[1] = packed
    got2[0:2] = packed

    def send_second(i, carry):
        ks = i ^ FAR
        send_sums(1, ((tm + 1) & 3, sp ^ ks), TILES + ks, got2)

        @pl.when(ks != 0)
        def _():
            send_sums(1, (tm, sp ^ ks), ks, got2)

        return carry

    lax.fori_loop(0, TILES, send_second, 0)

    def wait_second(i, carry):
        tap_copies(i)[1].wait()
        return carry

    lax.fori_loop(0, 27, wait_second, 0)
    sums_copy(1, got2, 128).wait_recv()

    stats_own = group_stats(got2[0:64], TILES * 64 * 16)
    stats_before = group_stats(got2[64:128], TILES * 64 * 16)
    pair = []
    for which in range(2):
        rows = by_frame(stats_before[which], stats_own[which], (0, 0, 1, 1, 1, 1, 1, 1), (2, 3, 0, 1, 2, 3, 3, 3))
        rows = jnp.where(starting & (row8 < 2), jnp.broadcast_to(rows[2:3], (8, LANES)), rows)
        pair.append(spread(rows))
    mean2, scale2 = pair[0], pair[1] * gain2[...]
    low4 = iota((1, 8, LANES), 1) < 4
    index9 = iota((9, 8, LANES), 0)
    for R in range(6):
        for k in range(CHUNKS):
            lanes = slice(k * LANES, (k + 1) * LANES)
            both = []
            for parity in range(2):
                v = (fs[R, parity, :, :, lanes] - mean2[:, lanes]) * scale2[:, lanes] + bias2[:, lanes]
                v = 0.5 * v * (1.0 + jnp.tanh(0.5 * v))
                outside = (rightmost & (index9 == 8)) if parity else (leftmost & (index9 == 0))
                if R == 0:
                    outside = outside | top
                if R == 5:
                    outside = outside | bottom
                both.append(jnp.where(outside, 0.0, v))
            for a in range(3):
                joined = []
                for parity in range(2):
                    lower, upper = both[parity][0:5], both[parity][4:9]
                    lower = sub_roll(lower, -a) if a else lower
                    joined.append(jnp.where(low4, lower, sub_roll(upper, 4 - a)))
                tile = jnp.concatenate(joined, axis=1).reshape(80, LANES).astype(BF16)
                actcat[80 * R : 80 * R + 80, a * C + k * LANES : a * C + (k + 1) * LANES] = tile

    def second_taps(e, carry):
        for b in range(3):
            begin, end = ((0, 400), (80, 400), (80, 480))[b]
            t2[b, e, begin:end] = jnp.dot(actcat[begin:end], w2[3 * b + e], preferred_element_type=F32)
        return carry

    lax.fori_loop(0, 3, second_taps, 0)

    to, fro = iota((128, 128), 0), iota((128, 128), 1)
    place_f, place_col = to >> 5, to & 31
    j = place_col >> 1
    source = (place_col & 1) * 64 + (j & 7) * 8 + (j >> 3) * 4 + place_f
    shuffle = jnp.where(fro == source, 1.0, 0.0).astype(BF16)
    for row in range(8):
        R = row // 2 + 1
        s = []
        for e in range(3):
            picks = (R - 1, R, R) if row % 2 == 0 else (R, R, R + 1)
            terms = [t2[b, e, 80 * at : 80 * at + 80].reshape(10, 8, C2) for b, at in enumerate(picks)]
            s.append(terms[0] + terms[1] + terms[2])
        q0 = s[0][0:8] + s[1][1:9] + s[2][1:9] + b2[...]
        q1 = s[0][1:9] + s[1][1:9] + s[2][2:10] + b2[...]
        stacked = jnp.concatenate([q0.reshape(64, C2), q1.reshape(64, C2)], axis=0).astype(BF16)
        final = jnp.dot(shuffle, stacked, preferred_element_type=F32).astype(BF16)
        for f in range(FRAMES):
            out_ref[f, row] = final[32 * f : 32 * f + 32]

    for dt in range(SHARDS):
        @pl.when(tm + dt < SHARDS)
        def _(dt=dt):
            block_copy(dt).wait_send()
    sums_copy(0, got1, 256).wait_send()
    sums_copy(1, got2, 128).wait_send()


def per_device(
    hidden_state, norm1_gain, norm1_bias, qkv_weight, out_weight, out_bias, conv1_weight, conv1_bias,
    norm2_gain, norm2_bias, conv2_weight, conv2_bias,
):
    any_spec = pl.BlockSpec(memory_space=pl.ANY)
    decoded = pl.pallas_call(
        kernel,
        out_shape=jax.ShapeDtypeStruct((FRAMES, 8, 32, C2), BF16),
        in_specs=[any_spec] * 12,
        out_specs=pl.BlockSpec(memory_space=pltpu.VMEM),
        scratch_shapes=[
            pltpu.VMEM((FRAMES, 2, 8, C), BF16),
            pltpu.VMEM((1, C), F32),
            pltpu.VMEM((1, C), F32),
            pltpu.VMEM((C, 3 * C), BF16),
            pltpu.VMEM((C, C), BF16),
            pltpu.VMEM((1, C), F32),
            pltpu.VMEM((9, 3 * C, C), BF16),
            pltpu.VMEM((1, C), F32),
            pltpu.VMEM((1, C), F32),
            pltpu.VMEM((1, C), F32),
            pltpu.VMEM((9, 3 * C, C2), BF16),
            pltpu.VMEM((1, C2), F32),
            pltpu.VMEM((64, C), BF16),
            pltpu.VMEM((2, 16, C), BF16),
            pltpu.VMEM((4, BLOCK_ROWS, C), BF16),
            pltpu.VMEM((2, 2, LANES), F32),
            pltpu.VMEM((256, LANES), F32),
            pltpu.VMEM((128, LANES), F32),
            pltpu.VMEM((CELLS, 8, C), F32),
            pltpu.VMEM((CELLS, 16, C), BF16),
            pltpu.VMEM((CELLS * 8, C), BF16),
            pltpu.VMEM((CELLS * 16, C), BF16),
            pltpu.VMEM((CELLS * 16, C), BF16),
            pltpu.VMEM((CELLS * 8, C), BF16),
            pltpu.VMEM((CELLS * 8, 3 * C), BF16),
            pltpu.VMEM((3, 3, CELLS * 8, C), F32),
            pltpu.VMEM((6, 2, 9, 8, C), F32),
            pltpu.VMEM((480, 3 * C), BF16),
            pltpu.VMEM((3, 3, 480, C2), F32),
            pltpu.SemaphoreType.DMA((10,)),
            pltpu.SemaphoreType.DMA((27,)),
            pltpu.SemaphoreType.DMA((27,)),
            pltpu.SemaphoreType.DMA((SHARDS,)),
            pltpu.SemaphoreType.DMA((SHARDS,)),
            pltpu.SemaphoreType.DMA((2,)),
            pltpu.SemaphoreType.DMA((2,)),
        ],
        compiler_params=pltpu.CompilerParams(collective_id=0, has_side_effects=True, vmem_limit_bytes=60 << 20),
    )(
        hidden_state.reshape(FRAMES, 2, 8, C),
        norm1_gain.reshape(1, C),
        norm1_bias.reshape(1, C),
        qkv_weight,
        out_weight,
        out_bias.reshape(1, C),
        conv1_weight.reshape(27, C, C),
        conv1_bias.reshape(1, C),
        norm2_gain.reshape(1, C),
        norm2_bias.reshape(1, C),
        conv2_weight.reshape(27, C, C2),
        conv2_bias.reshape(1, C2),
    )
    return decoded[:, None]


def solution(mesh):
    return jax.shard_map(
        per_device,
        mesh=mesh,
        in_specs=(P("tm", "space", None, None, None),) + (P(),) * 11,
        out_specs=P("tm", "space", None, None, None),
        check_vma=False,
    )
```

```python
import jax
import jax.numpy as jnp
from jax import lax
from jax.experimental import pallas as pl
from jax.experimental.pallas import tpu as pltpu
from jax.sharding import PartitionSpec as P

F32, BF16 = jnp.float32, jnp.bfloat16
MESH = pl.DeviceIdType.MESH
C, C2, LANES = 512, 256, 128
CHUNKS = C // LANES
GRID_COLS, GRID_ROWS, TILES, SHARDS = 4, 8, 32, 4
FRAMES = 4
CELLS = 40

def hops(kt, ks):
    return sum((0, 1, 2, 1)[v] for v in (ks >> 3, (ks >> 1) & 3, (ks & 1) * 2 + (kt >> 1)))


PEERS = sorted(((kt, ks) for kt in range(SHARDS) for ks in range(TILES) if kt or ks), key=lambda p: -hops(*p))
EPS = 1e-6
RING = ((-1, -1), (-1, 1), (1, -1), (1, 1), (-1, 0), (1, 0), (0, -1), (0, 1))
RING_ROWS = (16, 16, 16, 16, 128, 128, 32, 32)
RING_AT = (576, 592, 608, 624, 256, 384, 512, 544)
BLOCK_ROWS = 640


def iota(shape, axis):
    return lax.broadcasted_iota(jnp.int32, shape, axis)


def lane_roll(value, shift):
    return pltpu.roll(value, shift % LANES, axis=value.ndim - 1)


def sub_roll(value, shift):
    return pltpu.roll(value, shift % 8, axis=value.ndim - 2)


def by_chunk(value, rows):
    parts = [
        value[i : i + rows, k * LANES : (k + 1) * LANES] for i in range(0, value.shape[0], rows) for k in range(CHUNKS)
    ]
    return jnp.concatenate(parts, axis=0)


def pack_sums(total, first_row):
    lane = iota((8, LANES), 1)
    row = iota((8, LANES), 0)
    merged = jnp.zeros((8, LANES), F32)
    for k in range(CHUNKS):
        part = total[:, k * LANES : (k + 1) * LANES]
        for step in (1, 2, 4, 8):
            part = part + lane_roll(part, -step)
        part = jnp.where((lane & 15) == 0, part, 0.0)
        merged = merged + (lane_roll(part, k) if k else part)
    placed = jnp.zeros((8, LANES), F32)
    for f in range(FRAMES):
        placed = placed + jnp.where(row == first_row + f, lane_roll(merged, 4 * f) if f else merged, 0.0)
    return jnp.sum(placed, axis=0, keepdims=True)


def group_stats(block, count):
    total = jnp.sum(block.reshape(8, 8, LANES), axis=0)
    total = total + sub_roll(total, 2)
    total = total + sub_roll(total, 4)
    mean = total[0:1] * (1.0 / count)
    square = total[1:2] * (1.0 / count)
    scale = lax.rsqrt(square - mean * mean + EPS)
    return jnp.broadcast_to(mean, (8, LANES)), jnp.broadcast_to(scale, (8, LANES))


def by_frame(first, second, second_rows, frames):
    row = iota((8, LANES), 0)
    out = jnp.zeros((8, LANES), F32)
    for f in range(FRAMES):
        moved = (lane_roll(first, -4 * f), lane_roll(second, -4 * f)) if f else (first, second)
        for r in range(8):
            if frames[r] == f:
                out = jnp.where(row == r, moved[1] if second_rows[r] else moved[0], out)
    return out


def spread(rows):
    lane = iota((8, LANES), 1)
    parts = []
    for k in range(CHUNKS):
        part = jnp.where((lane & 15) == 0, lane_roll(rows, -k) if k else rows, 0.0)
        for step in (1, 2, 4, 8):
            part = part + lane_roll(part, step)
        parts.append(part)
    return jnp.concatenate(parts, axis=1)


def kernel(
    hid_hbm, gain1_hbm, bias1_hbm, wqkv_hbm, wout_hbm, bout_hbm, w1_hbm, b1_hbm, gain2_hbm, bias2_hbm, w2_hbm, b2_hbm,
    out_ref,
    hid, gain1, bias1, wqkv, wout, bout, w1, b1, gain2, bias2, w2, b2,
    side, hbuf, sums, got1, got2, xhi, normed, queries, keys, values, attended, mixcat, t1, fs, actcat, t2,
    small_sem, w1_sem, w2_sem, hid_send, hid_recv, pass_send, sum_send, sum_recv,
):
    tm = lax.axis_index("tm")
    sp = lax.axis_index("space")
    tile_row, tile_col = sp >> 2, sp & 3

    smalls = [
        pltpu.make_async_copy(a, b, small_sem.at[i])
        for i, (a, b) in enumerate(
            (
                (hid_hbm, hid), (wqkv_hbm, wqkv), (wout_hbm, wout), (gain1_hbm, gain1), (bias1_hbm, bias1),
                (bout_hbm, bout), (b1_hbm, b1), (gain2_hbm, gain2), (bias2_hbm, bias2), (b2_hbm, b2),
            )
        )
    ]
    for copy in smalls:
        copy.start()

    barrier = pltpu.get_barrier_semaphore()
    for kt, ks in PEERS:
        pl.semaphore_signal(barrier, inc=1, device_id=(tm ^ kt, sp ^ ks), device_id_type=MESH)

    def tap_copies(i):
        a, be = i // 9, lax.rem(i, 9)
        rows = pl.ds(pl.multiple_of(a * C, C), C)
        return (
            pltpu.make_async_copy(w1_hbm.at[i], w1.at[be, rows], w1_sem.at[i]),
            pltpu.make_async_copy(w2_hbm.at[i], w2.at[be, rows], w2_sem.at[i]),
        )

    def start_first(i, carry):
        tap_copies(i)[0].start()
        return carry

    def start_second(i, carry):
        tap_copies(i)[1].start()
        return carry

    lax.fori_loop(0, 27, start_first, 0)
    lax.fori_loop(0, 27, start_second, 0)

    for dt in range(1, SHARDS):
        @pl.when(tm < dt)
        def _():
            hbuf[3 - dt] = jnp.zeros((BLOCK_ROWS, LANES), BF16)

    for copy in smalls:
        copy.wait()
    order_out, order_in = iota((64, 64), 0), iota((64, 64), 1)
    wanted = (order_out & 3) * 16 + (order_out >> 2)
    permute = jnp.where(order_in == wanted, 1.0, 0.0).astype(BF16)
    plain = hid[...].astype(F32).reshape(64, C).astype(BF16)
    mine = jnp.dot(permute, plain, preferred_element_type=F32)
    hbuf[3, 0:256] = by_chunk(mine, 32).astype(BF16)
    low2 = iota((8, LANES), 0) < 4
    edges = (
        jnp.where(iota((8, C), 0) < 4, mine[0:8], sub_roll(mine[32:40], 4)),
        jnp.where(iota((8, C), 0) < 4, sub_roll(mine[24:32], 4), mine[56:64]),
    )
    for i, edge in enumerate(edges):
        side[32 * i : 32 * i + 32] = by_chunk(edge, 8).astype(BF16)
        chunk = [edge[:, k * LANES : (k + 1) * LANES] for k in range(CHUNKS)]
        upper = [jnp.where(low2, chunk[k], sub_roll(chunk[k + 1], 4)) for k in (0, 2)]
        lower = [jnp.where(low2, sub_roll(chunk[k], 4), chunk[k + 1]) for k in (0, 2)]
        side[64 + 16 * i : 80 + 16 * i] = jnp.concatenate(upper, axis=0).astype(BF16)
        side[96 + 16 * i : 112 + 16 * i] = jnp.concatenate(lower, axis=0).astype(BF16)
    pairs = mine.reshape(8, 8, C)
    first = jnp.sum(pairs, axis=0)
    second = jnp.sum(pairs * pairs, axis=0)
    first = first + sub_roll(first, 4)
    second = second + sub_roll(second, 4)
    packed = jnp.concatenate([pack_sums(first, 0), pack_sums(second, 0)], axis=0)
    sums[0] = packed
    got1[0:2] = packed

    pl.semaphore_wait(barrier, SHARDS * TILES - 1)

    def send_sums(which, target, slot, buf):
        pltpu.make_async_remote_copy(
            src_ref=sums.at[which], dst_ref=buf.at[pl.ds(pl.multiple_of(slot * 2, 2), 2)],
            send_sem=sum_send.at[which], recv_sem=sum_recv.at[which], device_id=target, device_id_type=MESH,
        ).start()

    for kt, ks in PEERS:
        send_sums(0, (tm ^ kt, sp ^ ks), kt * TILES + ks, got1)

    def piece(dr, dc):
        if dc == 0:
            return hbuf.at[3, pl.ds(0, 128)] if dr < 0 else hbuf.at[3, pl.ds(128, 128)]
        column = 0 if dc < 0 else 1
        if dr == 0:
            return side.at[pl.ds(32 * column, 32)]
        return side.at[pl.ds((64 if dr < 0 else 96) + 16 * column, 16)]

    def ring_push(dt):
        def push(src, at, rows, target):
            pltpu.make_async_remote_copy(
                src_ref=src, dst_ref=hbuf.at[3 - dt, pl.ds(at, rows)], send_sem=hid_send.at[dt],
                recv_sem=hid_recv.at[dt], device_id=target, device_id_type=MESH,
            ).start()

        for i, (dr, dc) in enumerate(RING):
            there = ((tile_row + dr) & 7) * GRID_COLS + ((tile_col + dc) & 3)
            push(piece(dr, dc), RING_AT[RING.index((-dr, -dc))], RING_ROWS[i], (tm + dt, there))
        if dt:
            push(hbuf.at[3, pl.ds(0, 256)], 0, 256, (tm + dt, sp))

    ring_push(0)
    pl.when(tm < 2)(lambda: ring_push(2))

    def block_copy(dt):
        ref = hbuf.at[3, pl.ds(256, 384)] if dt == 0 else hbuf.at[3 - dt]
        return pltpu.make_async_remote_copy(
            src_ref=ref, dst_ref=ref, send_sem=hid_send.at[dt], recv_sem=hid_recv.at[dt],
            device_id=(tm ^ 1, sp), device_id_type=MESH,
        )

    def forward(here, there):
        return pltpu.make_async_remote_copy(
            src_ref=hbuf.at[3 - here], dst_ref=hbuf.at[3 - there], send_sem=pass_send.at[here // 2],
            recv_sem=hid_recv.at[there], device_id=(tm ^ 1, sp), device_id_type=MESH,
        )

    def sums_copy(which, buf, rows):
        ref = buf.at[pl.ds(2, rows - 2)]
        return pltpu.make_async_remote_copy(
            src_ref=ref, dst_ref=ref, send_sem=sum_send.at[which], recv_sem=sum_recv.at[which],
            device_id=(tm ^ 1, sp), device_id_type=MESH,
        )

    first_core = (tm & 1) == 0
    block_copy(0).wait_recv()
    pl.when(first_core)(lambda: forward(0, 1).start())

    @pl.when(tm >= 2)
    def _():
        block_copy(2).wait_recv()
        pl.when(first_core)(lambda: forward(2, 3).start())
        pl.when(jnp.logical_not(first_core))(lambda: forward(2, 1).start())

    pl.when(tm >= 1)(lambda: block_copy(1).wait_recv())
    pl.when(tm == 3)(lambda: block_copy(3).wait_recv())

    sums_copy(0, got1, 256).wait_recv()

    starting = tm == 0
    row8 = iota((8, LANES), 0)
    stats = []
    for dt in range(SHARDS):
        kt = tm ^ ((tm - dt) & 3)
        stats.append(group_stats(got1[pl.ds(pl.multiple_of(kt * 64, 64), 64)], TILES * 16 * 16))
    span = (0, 0, 0, 0, 1, 1, 1, 1)
    steps = (0, 1, 2, 3, 0, 1, 2, 3)
    normers = []
    for half in range(2):
        pair = []
        for which in range(2):
            rows = by_frame(stats[3 - 2 * half][which], stats[2 - 2 * half][which], span, steps)
            if half:
                rows = jnp.where(starting & (row8 < 4), jnp.broadcast_to(rows[4:5], (8, LANES)), rows)
            pair.append(spread(rows))
        normers.append((pair[0], pair[1] * gain1[...]))
    shift1 = bias1[...]
    low = iota((1, 8, C), 1) < 4

    def place(cells, parts, odd):
        halves = []
        for half in range(2):
            a, b = parts[2 * half], parts[2 * half + 1]
            if odd:
                a = sub_roll(a, 4)
            else:
                b = sub_roll(b, 4)
            halves.append(jnp.where(low, a, b))
        lo, hi = halves
        hi = jnp.where(starting & low, jnp.broadcast_to(hi[:, 4:5], hi.shape), hi)
        nlo = (lo - normers[0][0]) * normers[0][1] + shift1
        nhi = (hi - normers[1][0]) * normers[1][1] + shift1
        for i, cell in enumerate(cells):
            xhi[cell] = hi[i]
            normed[cell] = jnp.concatenate([nlo[i], nhi[i]], axis=0).astype(BF16)

    def rows_of(at, rows):
        out = []
        for s in range(4):
            value = hbuf[s, at : at + CHUNKS * rows].astype(F32)
            value = jnp.concatenate([value[k * rows : (k + 1) * rows] for k in range(CHUNKS)], axis=1)
            out.append(value.reshape(rows // 8, 8, C))
        return out

    def corner_of(at):
        out = []
        for s in range(4):
            value = hbuf[s, at : at + 16].astype(F32)
            halves = (value[0:8], value[8:16])
            value = jnp.concatenate([sub_roll(halves[k // 2], 4 * (k & 1)) if k & 1 else halves[k // 2] for k in range(CHUNKS)], axis=1)
            out.append(value.reshape(1, 8, C))
        return out

    for r in range(4):
        parts = rows_of((256, 0, 128, 384)[r], 32)
        for odd in range(2):
            place([r * 10 + 1 + 2 * i + odd for i in range(4)], parts, odd)
    for at, column in ((512, 0), (544, 9)):
        parts = rows_of(at, 8)
        place([10 + column], parts, 0)
        place([20 + column], parts, 1)
    for i, cell in enumerate((0, 9, 30, 39)):
        place([cell], corner_of(RING_AT[i]), 0)

    for g in range(20):
        two = normed[2 * g : 2 * g + 2].astype(F32)
        queries[16 * g : 16 * g + 16] = jnp.concatenate([two[0, 8:16], two[1, 8:16]], axis=0).astype(BF16)
    asked = jnp.dot(queries[...], wqkv[:, 0:C], preferred_element_type=F32)
    queries[...] = asked.astype(BF16)
    everything = normed[...].reshape(CELLS * 16, C)
    keys[...] = jnp.dot(everything, wqkv[:, C : 2 * C], preferred_element_type=F32).astype(BF16)
    values[...] = jnp.dot(everything, wqkv[:, 2 * C :], preferred_element_type=F32).astype(BF16)

    q_row, k_col = iota((64, 128), 0), iota((64, 128), 1)
    first_frame = 12 - 4 * tm
    q_frame = jnp.maximum((q_row & 7) + 8, first_frame)
    k_frame = k_col & 15
    allowed = ((q_row >> 3) == (k_col >> 4)) & (k_frame <= q_frame) & (k_frame >= first_frame)
    for g in range(5):
        q = queries[64 * g : 64 * g + 64]
        k = keys[128 * g : 128 * g + 128]
        v = values[128 * g : 128 * g + 128]
        scores = lax.dot_general(q, k, (((1,), (1,)), ((), ())), preferred_element_type=F32) * C ** (-0.5)
        scores = jnp.where(allowed, scores, -1e30)
        weights = jnp.exp(scores - jnp.max(scores, axis=1, keepdims=True))
        weights = jnp.where(allowed, weights, 0.0)
        total = jnp.sum(weights, axis=1, keepdims=True)
        summed = jnp.dot(weights.astype(BF16), v, preferred_element_type=F32)
        attended[64 * g : 64 * g + 64] = (summed / total).astype(BF16)

    projected = jnp.dot(attended[...], wout[...], preferred_element_type=F32).reshape(CELLS, 8, C)
    top, bottom = tile_row == 0, tile_row == GRID_ROWS - 1
    leftmost, rightmost = tile_col == 0, tile_col == GRID_COLS - 1
    for r in range(4):
        mixed = (xhi[10 * r : 10 * r + 10] + (projected[10 * r : 10 * r + 10] + bout[...])).astype(BF16).astype(F32)
        col = iota((10, 8, C), 0)
        outside = (leftmost & (col == 0)) | (rightmost & (col == 9))
        if r == 0:
            outside = outside | top
        if r == 3:
            outside = outside | bottom
        mixed = jnp.where(outside, 0.0, mixed)
        for a in range(3):
            moved = sub_roll(mixed, -a) if a else mixed
            mixcat[80 * r : 80 * r + 80, a * C : (a + 1) * C] = moved.reshape(80, C).astype(BF16)

    def wait_first(i, carry):
        tap_copies(i)[0].wait()
        return carry

    lax.fori_loop(0, 27, wait_first, 0)

    def first_taps(e, carry):
        for b in range(3):
            begin, end = ((0, 240), (0, 320), (80, 320))[b]
            t1[b, e, begin:end] = jnp.dot(mixcat[begin:end], w1[3 * b + e], preferred_element_type=F32)
        return carry

    lax.fori_loop(0, 3, first_taps, 0)

    def t1_row(b, e, r, lanes):
        return t1[b, e, 80 * r : 80 * r + 80, lanes].reshape(10, 8, LANES)

    sum_first, sum_second = [], []
    for k in range(CHUNKS):
        lanes = slice(k * LANES, (k + 1) * LANES)
        acc, acc2 = jnp.zeros((8, LANES), F32), jnp.zeros((8, LANES), F32)
        for R in range(6):
            s = []
            for e in range(3):
                if R % 2 == 0:
                    r = R // 2
                    s.append(t1_row(0, e, r, lanes) + t1_row(1, e, r, lanes) + t1_row(2, e, r + 1, lanes))
                else:
                    r = (R + 1) // 2
                    s.append(t1_row(0, e, r - 1, lanes) + t1_row(1, e, r, lanes) + t1_row(2, e, r, lanes))
            even = s[0][0:9] + s[1][0:9] + s[2][1:10] + b1[:, lanes]
            odd = s[0][0:9] + s[1][1:10] + s[2][1:10] + b1[:, lanes]
            even = even.astype(BF16).astype(F32)
            odd = odd.astype(BF16).astype(F32)
            fs[R, 0, :, :, lanes] = even
            fs[R, 1, :, :, lanes] = odd
            if 1 <= R <= 4:
                inner_e, inner_o = even[1:9], odd[0:8]
                acc = acc + jnp.sum(inner_e, axis=0) + jnp.sum(inner_o, axis=0)
                acc2 = acc2 + jnp.sum(inner_e * inner_e, axis=0) + jnp.sum(inner_o * inner_o, axis=0)
        sum_first.append(acc)
        sum_second.append(acc2)
    packed = jnp.concatenate(
        [pack_sums(jnp.concatenate(sum_first, axis=1), 2), pack_sums(jnp.concatenate(sum_second, axis=1), 2)], axis=0
    )
    sums[1] = packed
    got2[0:2] = packed

    for kt, ks in PEERS:
        if kt == 0:
            send_sums(1, (tm, sp ^ ks), ks, got2)
        if kt == 1:
            send_sums(1, ((tm + 1) & 3, sp ^ ks), TILES + ks, got2)

    def wait_second(i, carry):
        tap_copies(i)[1].wait()
        return carry

    lax.fori_loop(0, 27, wait_second, 0)
    sums_copy(1, got2, 128).wait_recv()

    stats_own = group_stats(got2[0:64], TILES * 64 * 16)
    stats_before = group_stats(got2[64:128], TILES * 64 * 16)
    pair = []
    for which in range(2):
        rows = by_frame(stats_before[which], stats_own[which], (0, 0, 1, 1, 1, 1, 1, 1), (2, 3, 0, 1, 2, 3, 3, 3))
        rows = jnp.where(starting & (row8 < 2), jnp.broadcast_to(rows[2:3], (8, LANES)), rows)
        pair.append(spread(rows))
    mean2, scale2 = pair[0], pair[1] * gain2[...]
    low4 = iota((1, 8, LANES), 1) < 4
    index9 = iota((9, 8, LANES), 0)
    for R in range(6):
        for k in range(CHUNKS):
            lanes = slice(k * LANES, (k + 1) * LANES)
            both = []
            for parity in range(2):
                v = (fs[R, parity, :, :, lanes] - mean2[:, lanes]) * scale2[:, lanes] + bias2[:, lanes]
                v = 0.5 * v * (1.0 + jnp.tanh(0.5 * v))
                outside = (rightmost & (index9 == 8)) if parity else (leftmost & (index9 == 0))
                if R == 0:
                    outside = outside | top
                if R == 5:
                    outside = outside | bottom
                both.append(jnp.where(outside, 0.0, v))
            for a in range(3):
                joined = []
                for parity in range(2):
                    lower, upper = both[parity][0:5], both[parity][4:9]
                    lower = sub_roll(lower, -a) if a else lower
                    joined.append(jnp.where(low4, lower, sub_roll(upper, 4 - a)))
                tile = jnp.concatenate(joined, axis=1).reshape(80, LANES).astype(BF16)
                actcat[80 * R : 80 * R + 80, a * C + k * LANES : a * C + (k + 1) * LANES] = tile

    def second_taps(e, carry):
        for b in range(3):
            begin, end = ((0, 400), (80, 400), (80, 480))[b]
            t2[b, e, begin:end] = jnp.dot(actcat[begin:end], w2[3 * b + e], preferred_element_type=F32)
        return carry

    lax.fori_loop(0, 3, second_taps, 0)

    to, fro = iota((128, 128), 0), iota((128, 128), 1)
    place_f, place_col = to >> 5, to & 31
    j = place_col >> 1
    source = (place_col & 1) * 64 + (j & 7) * 8 + (j >> 3) * 4 + place_f
    shuffle = jnp.where(fro == source, 1.0, 0.0).astype(BF16)
    for row in range(8):
        R = row // 2 + 1
        s = []
        for e in range(3):
            picks = (R - 1, R, R) if row % 2 == 0 else (R, R, R + 1)
            terms = [t2[b, e, 80 * at : 80 * at + 80].reshape(10, 8, C2) for b, at in enumerate(picks)]
            s.append(terms[0] + terms[1] + terms[2])
        q0 = s[0][0:8] + s[1][1:9] + s[2][1:9] + b2[...]
        q1 = s[0][1:9] + s[1][1:9] + s[2][2:10] + b2[...]
        stacked = jnp.concatenate([q0.reshape(64, C2), q1.reshape(64, C2)], axis=0).astype(BF16)
        final = jnp.dot(shuffle, stacked, preferred_element_type=F32).astype(BF16)
        for f in range(FRAMES):
            out_ref[f, row] = final[32 * f : 32 * f + 32]

    block_copy(0).wait_send()
    pl.when(tm < 2)(lambda: block_copy(2).wait_send())
    pl.when(first_core)(lambda: forward(0, 1).wait_send())
    pl.when(tm >= 2)(lambda: forward(2, 1).wait_send())
    sums_copy(0, got1, 256).wait_send()
    sums_copy(1, got2, 128).wait_send()


def per_device(
    hidden_state, norm1_gain, norm1_bias, qkv_weight, out_weight, out_bias, conv1_weight, conv1_bias,
    norm2_gain, norm2_bias, conv2_weight, conv2_bias,
):
    any_spec = pl.BlockSpec(memory_space=pl.ANY)
    decoded = pl.pallas_call(
        kernel,
        out_shape=jax.ShapeDtypeStruct((FRAMES, 8, 32, C2), BF16),
        in_specs=[any_spec] * 12,
        out_specs=pl.BlockSpec(memory_space=pltpu.VMEM),
        scratch_shapes=[
            pltpu.VMEM((FRAMES, 2, 8, C), BF16),
            pltpu.VMEM((1, C), F32),
            pltpu.VMEM((1, C), F32),
            pltpu.VMEM((C, 3 * C), BF16),
            pltpu.VMEM((C, C), BF16),
            pltpu.VMEM((1, C), F32),
            pltpu.VMEM((9, 3 * C, C), BF16),
            pltpu.VMEM((1, C), F32),
            pltpu.VMEM((1, C), F32),
            pltpu.VMEM((1, C), F32),
            pltpu.VMEM((9, 3 * C, C2), BF16),
            pltpu.VMEM((1, C2), F32),
            pltpu.VMEM((128, LANES), BF16),
            pltpu.VMEM((4, BLOCK_ROWS, LANES), BF16),
            pltpu.VMEM((2, 2, LANES), F32),
            pltpu.VMEM((256, LANES), F32),
            pltpu.VMEM((128, LANES), F32),
            pltpu.VMEM((CELLS, 8, C), F32),
            pltpu.VMEM((CELLS, 16, C), BF16),
            pltpu.VMEM((CELLS * 8, C), BF16),
            pltpu.VMEM((CELLS * 16, C), BF16),
            pltpu.VMEM((CELLS * 16, C), BF16),
            pltpu.VMEM((CELLS * 8, C), BF16),
            pltpu.VMEM((CELLS * 8, 3 * C), BF16),
            pltpu.VMEM((3, 3, CELLS * 8, C), F32),
            pltpu.VMEM((6, 2, 9, 8, C), F32),
            pltpu.VMEM((480, 3 * C), BF16),
            pltpu.VMEM((3, 3, 480, C2), F32),
            pltpu.SemaphoreType.DMA((10,)),
            pltpu.SemaphoreType.DMA((27,)),
            pltpu.SemaphoreType.DMA((27,)),
            pltpu.SemaphoreType.DMA((SHARDS,)),
            pltpu.SemaphoreType.DMA((SHARDS,)),
            pltpu.SemaphoreType.DMA((2,)),
            pltpu.SemaphoreType.DMA((2,)),
            pltpu.SemaphoreType.DMA((2,)),
        ],
        compiler_params=pltpu.CompilerParams(collective_id=0, has_side_effects=True, vmem_limit_bytes=60 << 20),
    )(
        hidden_state.reshape(FRAMES, 2, 8, C),
        norm1_gain.reshape(1, C),
        norm1_bias.reshape(1, C),
        qkv_weight,
        out_weight,
        out_bias.reshape(1, C),
        conv1_weight.reshape(27, C, C),
        conv1_bias.reshape(1, C),
        norm2_gain.reshape(1, C),
        norm2_bias.reshape(1, C),
        conv2_weight.reshape(27, C, C2),
        conv2_bias.reshape(1, C2),
    )
    return decoded[:, None]


def solution(mesh):
    return jax.shard_map(
        per_device,
        mesh=mesh,
        in_specs=(P("tm", "space", None, None, None),) + (P(),) * 11,
        out_specs=P("tm", "space", None, None, None),
        check_vma=False,
    )
```

```python
import jax
import jax.numpy as jnp
from jax import lax
from jax.experimental import pallas as pl
from jax.experimental.pallas import tpu as pltpu
from jax.sharding import PartitionSpec as P

F32, BF16 = jnp.float32, jnp.bfloat16
MESH = pl.DeviceIdType.MESH
C, C2, LANES = 512, 256, 128
CHUNKS = C // LANES
GRID_COLS, GRID_ROWS, TILES, SHARDS = 4, 8, 32, 4
FRAMES = 4
CELLS = 40

def hops(kt, ks):
    return sum((0, 1, 2, 1)[v] for v in (ks >> 3, (ks >> 1) & 3, (ks & 1) * 2 + (kt >> 1)))


PEERS = sorted(((kt, ks) for kt in range(SHARDS) for ks in range(TILES) if kt or ks), key=lambda p: -hops(*p))
EPS = 1e-6
RING = ((-1, -1), (-1, 1), (1, -1), (1, 1), (-1, 0), (1, 0), (0, -1), (0, 1))
RING_ROWS = (16, 16, 16, 16, 128, 128, 32, 32)
RING_AT = (576, 592, 608, 624, 256, 384, 512, 544)
BLOCK_ROWS = 640


def iota(shape, axis):
    return lax.broadcasted_iota(jnp.int32, shape, axis)


def lane_roll(value, shift):
    return pltpu.roll(value, shift % LANES, axis=value.ndim - 1)


def sub_roll(value, shift):
    return pltpu.roll(value, shift % 8, axis=value.ndim - 2)


def by_chunk(value, rows):
    parts = [
        value[i : i + rows, k * LANES : (k + 1) * LANES] for i in range(0, value.shape[0], rows) for k in range(CHUNKS)
    ]
    return jnp.concatenate(parts, axis=0)


def pack_sums(total, first_row):
    lane = iota((8, LANES), 1)
    row = iota((8, LANES), 0)
    merged = jnp.zeros((8, LANES), F32)
    for k in range(CHUNKS):
        part = total[:, k * LANES : (k + 1) * LANES]
        for step in (1, 2, 4, 8):
            part = part + lane_roll(part, -step)
        part = jnp.where((lane & 15) == 0, part, 0.0)
        merged = merged + (lane_roll(part, k) if k else part)
    placed = jnp.zeros((8, LANES), F32)
    for f in range(FRAMES):
        placed = placed + jnp.where(row == first_row + f, lane_roll(merged, 4 * f) if f else merged, 0.0)
    return jnp.sum(placed, axis=0, keepdims=True)


def group_stats(block, count):
    total = jnp.sum(block.reshape(8, 8, LANES), axis=0)
    total = total + sub_roll(total, 2)
    total = total + sub_roll(total, 4)
    mean = total[0:1] * (1.0 / count)
    square = total[1:2] * (1.0 / count)
    scale = lax.rsqrt(square - mean * mean + EPS)
    return jnp.broadcast_to(mean, (8, LANES)), jnp.broadcast_to(scale, (8, LANES))


def by_frame(first, second, second_rows, frames):
    row = iota((8, LANES), 0)
    out = jnp.zeros((8, LANES), F32)
    for f in range(FRAMES):
        moved = (lane_roll(first, -4 * f), lane_roll(second, -4 * f)) if f else (first, second)
        for r in range(8):
            if frames[r] == f:
                out = jnp.where(row == r, moved[1] if second_rows[r] else moved[0], out)
    return out


def spread(rows):
    lane = iota((8, LANES), 1)
    parts = []
    for k in range(CHUNKS):
        part = jnp.where((lane & 15) == 0, lane_roll(rows, -k) if k else rows, 0.0)
        for step in (1, 2, 4, 8):
            part = part + lane_roll(part, step)
        parts.append(part)
    return jnp.concatenate(parts, axis=1)


def kernel(
    hid_hbm, gain1_hbm, bias1_hbm, wqkv_hbm, wout_hbm, bout_hbm, w1_hbm, b1_hbm, gain2_hbm, bias2_hbm, w2_hbm, b2_hbm,
    out_ref,
    hid, gain1, bias1, wqkv, wout, bout, w1, b1, gain2, bias2, w2, b2,
    side, hbuf, sums, got1, got2, xhi, normed, queries, keys, values, attended, mixcat, t1, fs, actcat, t2,
    small_sem, w1_sem, w2_sem, hid_send, hid_recv, pass_send, cen_send, cen_recv, cpass_send, sum_send, sum_recv,
):
    tm = lax.axis_index("tm")
    sp = lax.axis_index("space")
    tile_row, tile_col = sp >> 2, sp & 3

    smalls = [
        pltpu.make_async_copy(a, b, small_sem.at[i])
        for i, (a, b) in enumerate(
            (
                (hid_hbm, hid), (wqkv_hbm, wqkv), (wout_hbm, wout), (gain1_hbm, gain1), (bias1_hbm, bias1),
                (bout_hbm, bout), (b1_hbm, b1), (gain2_hbm, gain2), (bias2_hbm, bias2), (b2_hbm, b2),
            )
        )
    ]
    for copy in smalls:
        copy.start()

    barrier = pltpu.get_barrier_semaphore()
    for kt, ks in PEERS:
        pl.semaphore_signal(barrier, inc=1, device_id=(tm ^ kt, sp ^ ks), device_id_type=MESH)

    def tap_copies(i):
        a, be = i // 9, lax.rem(i, 9)
        rows = pl.ds(pl.multiple_of(a * C, C), C)
        return (
            pltpu.make_async_copy(w1_hbm.at[i], w1.at[be, rows], w1_sem.at[i]),
            pltpu.make_async_copy(w2_hbm.at[i], w2.at[be, rows], w2_sem.at[i]),
        )

    def start_first(i, carry):
        tap_copies(i)[0].start()
        return carry

    def start_second(i, carry):
        tap_copies(i)[1].start()
        return carry

    lax.fori_loop(0, 27, start_first, 0)
    lax.fori_loop(0, 27, start_second, 0)

    for dt in range(1, SHARDS):
        @pl.when(tm < dt)
        def _():
            hbuf[3 - dt] = jnp.zeros((BLOCK_ROWS, LANES), BF16)

    for copy in smalls:
        copy.wait()
    order_out, order_in = iota((64, 64), 0), iota((64, 64), 1)
    wanted = (order_out & 3) * 16 + (order_out >> 2)
    permute = jnp.where(order_in == wanted, 1.0, 0.0).astype(BF16)
    plain = hid[...].astype(F32).reshape(64, C).astype(BF16)
    mine = jnp.dot(permute, plain, preferred_element_type=F32)
    hbuf[3, 0:256] = by_chunk(mine, 32).astype(BF16)
    low2 = iota((8, LANES), 0) < 4
    edges = (
        jnp.where(iota((8, C), 0) < 4, mine[0:8], sub_roll(mine[32:40], 4)),
        jnp.where(iota((8, C), 0) < 4, sub_roll(mine[24:32], 4), mine[56:64]),
    )
    for i, edge in enumerate(edges):
        side[32 * i : 32 * i + 32] = by_chunk(edge, 8).astype(BF16)
        chunk = [edge[:, k * LANES : (k + 1) * LANES] for k in range(CHUNKS)]
        upper = [jnp.where(low2, chunk[k], sub_roll(chunk[k + 1], 4)) for k in (0, 2)]
        lower = [jnp.where(low2, sub_roll(chunk[k], 4), chunk[k + 1]) for k in (0, 2)]
        side[64 + 16 * i : 80 + 16 * i] = jnp.concatenate(upper, axis=0).astype(BF16)
        side[96 + 16 * i : 112 + 16 * i] = jnp.concatenate(lower, axis=0).astype(BF16)
    pairs = mine.reshape(8, 8, C)
    first = jnp.sum(pairs, axis=0)
    second = jnp.sum(pairs * pairs, axis=0)
    first = first + sub_roll(first, 4)
    second = second + sub_roll(second, 4)
    packed = jnp.concatenate([pack_sums(first, 0), pack_sums(second, 0)], axis=0)
    sums[0] = packed
    got1[0:2] = packed

    pl.semaphore_wait(barrier, SHARDS * TILES - 1)

    def send_sums(which, target, slot, buf):
        pltpu.make_async_remote_copy(
            src_ref=sums.at[which], dst_ref=buf.at[pl.ds(pl.multiple_of(slot * 2, 2), 2)],
            send_sem=sum_send.at[which], recv_sem=sum_recv.at[which], device_id=target, device_id_type=MESH,
        ).start()

    for kt, ks in PEERS:
        send_sums(0, (tm ^ kt, sp ^ ks), kt * TILES + ks, got1)

    def piece(dr, dc):
        if dc == 0:
            return hbuf.at[3, pl.ds(0, 128)] if dr < 0 else hbuf.at[3, pl.ds(128, 128)]
        column = 0 if dc < 0 else 1
        if dr == 0:
            return side.at[pl.ds(32 * column, 32)]
        return side.at[pl.ds((64 if dr < 0 else 96) + 16 * column, 16)]

    def ring_push(dt):
        def push(src, at, rows, target):
            pltpu.make_async_remote_copy(
                src_ref=src, dst_ref=hbuf.at[3 - dt, pl.ds(at, rows)], send_sem=hid_send.at[dt],
                recv_sem=hid_recv.at[dt], device_id=target, device_id_type=MESH,
            ).start()

        for i, (dr, dc) in enumerate(RING):
            there = ((tile_row + dr) & 7) * GRID_COLS + ((tile_col + dc) & 3)
            push(piece(dr, dc), RING_AT[RING.index((-dr, -dc))], RING_ROWS[i], (tm + dt, there))

    ring_push(0)
    pl.when(tm < 2)(lambda: ring_push(2))

    RING_PART, CENTRE = pl.ds(256, 384), pl.ds(0, 256)

    def block_copy(dt):
        ref = hbuf.at[3 - dt, RING_PART]
        return pltpu.make_async_remote_copy(
            src_ref=ref, dst_ref=ref, send_sem=hid_send.at[dt], recv_sem=hid_recv.at[dt],
            device_id=(tm ^ 1, sp), device_id_type=MESH,
        )

    def centre_copy(dt):
        return pltpu.make_async_remote_copy(
            src_ref=hbuf.at[3, CENTRE], dst_ref=hbuf.at[3 - dt, CENTRE], send_sem=cen_send.at[dt],
            recv_sem=cen_recv.at[dt], device_id=(tm + dt, sp), device_id_type=MESH,
        )

    def forward(here, there, part, sends, recvs):
        return pltpu.make_async_remote_copy(
            src_ref=hbuf.at[3 - here, part], dst_ref=hbuf.at[3 - there, part], send_sem=sends.at[here // 2],
            recv_sem=recvs.at[there], device_id=(tm ^ 1, sp), device_id_type=MESH,
        )

    def ring_forward(here, there):
        return forward(here, there, RING_PART, pass_send, hid_recv)

    def centre_forward(here, there):
        return forward(here, there, CENTRE, cpass_send, cen_recv)

    def sums_copy(which, buf, rows):
        ref = buf.at[pl.ds(2, rows - 2)]
        return pltpu.make_async_remote_copy(
            src_ref=ref, dst_ref=ref, send_sem=sum_send.at[which], recv_sem=sum_recv.at[which],
            device_id=(tm ^ 1, sp), device_id_type=MESH,
        )

    def pass_on(copy_in, passing):
        @pl.when(tm >= 2)
        def _():
            copy_in(2).wait_recv()
            pl.when(first_core)(lambda: passing(2, 3).start())
            pl.when(jnp.logical_not(first_core))(lambda: passing(2, 1).start())

    def await_passed(copy_in):
        pl.when(tm >= 1)(lambda: copy_in(1).wait_recv())
        pl.when(tm == 3)(lambda: copy_in(3).wait_recv())

    first_core = (tm & 1) == 0
    pl.when(tm < 2)(lambda: centre_copy(2).start())
    pl.when(first_core)(lambda: centre_forward(0, 1).start())
    pass_on(centre_copy, centre_forward)
    await_passed(centre_copy)
    sums_copy(0, got1, 256).wait_recv()

    starting = tm == 0
    row8 = iota((8, LANES), 0)
    stats = []
    for dt in range(SHARDS):
        kt = tm ^ ((tm - dt) & 3)
        stats.append(group_stats(got1[pl.ds(pl.multiple_of(kt * 64, 64), 64)], TILES * 16 * 16))
    span = (0, 0, 0, 0, 1, 1, 1, 1)
    steps = (0, 1, 2, 3, 0, 1, 2, 3)
    normers = []
    for half in range(2):
        pair = []
        for which in range(2):
            rows = by_frame(stats[3 - 2 * half][which], stats[2 - 2 * half][which], span, steps)
            if half:
                rows = jnp.where(starting & (row8 < 4), jnp.broadcast_to(rows[4:5], (8, LANES)), rows)
            pair.append(spread(rows))
        normers.append((pair[0], pair[1] * gain1[...]))
    shift1 = bias1[...]
    low = iota((1, 8, C), 1) < 4

    def place(cells, parts, odd):
        halves = []
        for half in range(2):
            a, b = parts[2 * half], parts[2 * half + 1]
            if odd:
                a = sub_roll(a, 4)
            else:
                b = sub_roll(b, 4)
            halves.append(jnp.where(low, a, b))
        lo, hi = halves
        hi = jnp.where(starting & low, jnp.broadcast_to(hi[:, 4:5], hi.shape), hi)
        nlo = (lo - normers[0][0]) * normers[0][1] + shift1
        nhi = (hi - normers[1][0]) * normers[1][1] + shift1
        for i, cell in enumerate(cells):
            xhi[cell] = hi[i]
            normed[cell] = jnp.concatenate([nlo[i], nhi[i]], axis=0).astype(BF16)

    def rows_of(at, rows):
        out = []
        for s in range(4):
            value = hbuf[s, at : at + CHUNKS * rows].astype(F32)
            value = jnp.concatenate([value[k * rows : (k + 1) * rows] for k in range(CHUNKS)], axis=1)
            out.append(value.reshape(rows // 8, 8, C))
        return out

    def corner_of(at):
        out = []
        for s in range(4):
            value = hbuf[s, at : at + 16].astype(F32)
            halves = (value[0:8], value[8:16])
            value = jnp.concatenate([sub_roll(halves[k // 2], 4 * (k & 1)) if k & 1 else halves[k // 2] for k in range(CHUNKS)], axis=1)
            out.append(value.reshape(1, 8, C))
        return out

    def line(at, cell):
        parts = rows_of(at, 32)
        for odd in range(2):
            place([cell + 2 * i + odd for i in range(4)], parts, odd)

    def project(begin, end):
        for g in range(begin // 2, end // 2):
            two = normed[2 * g : 2 * g + 2].astype(F32)
            queries[16 * g : 16 * g + 16] = jnp.concatenate([two[0, 8:16], two[1, 8:16]], axis=0).astype(BF16)
        asking, rows = slice(8 * begin, 8 * end), slice(16 * begin, 16 * end)
        queries[asking] = jnp.dot(queries[asking], wqkv[:, 0:C], preferred_element_type=F32).astype(BF16)
        part = normed[begin:end].reshape((end - begin) * 16, C)
        keys[rows] = jnp.dot(part, wqkv[:, C : 2 * C], preferred_element_type=F32).astype(BF16)
        values[rows] = jnp.dot(part, wqkv[:, 2 * C :], preferred_element_type=F32).astype(BF16)

    q_row, k_col = iota((64, 128), 0), iota((64, 128), 1)
    first_frame = 12 - 4 * tm
    q_frame = jnp.maximum((q_row & 7) + 8, first_frame)
    k_frame = k_col & 15
    allowed = ((q_row >> 3) == (k_col >> 4)) & (k_frame <= q_frame) & (k_frame >= first_frame)

    def attend(groups):
        scores = [
            lax.dot_general(
                queries[64 * g : 64 * g + 64], keys[128 * g : 128 * g + 128], (((1,), (1,)), ((), ())),
                preferred_element_type=F32,
            )
            for g in groups
        ]
        weights, totals = [], []
        for part in scores:
            part = jnp.where(allowed, part * C ** (-0.5), -1e30)
            part = jnp.exp(part - jnp.max(part, axis=1, keepdims=True))
            part = jnp.where(allowed, part, 0.0)
            totals.append(jnp.sum(part, axis=1, keepdims=True))
            weights.append(part.astype(BF16))
        summed = [
            jnp.dot(part, values[128 * g : 128 * g + 128], preferred_element_type=F32) for part, g in zip(weights, groups)
        ]
        for part, total, g in zip(summed, totals, groups):
            attended[64 * g : 64 * g + 64] = (part / total).astype(BF16)

    line(0, 0)
    line(128, 8)
    project(0, 16)
    block_copy(0).wait_recv()
    pl.when(first_core)(lambda: ring_forward(0, 1).start())
    pass_on(block_copy, ring_forward)
    attend((0, 1))
    await_passed(block_copy)
    line(256, 16)
    line(384, 24)
    for at, cell in ((512, 32), (544, 34)):
        parts = rows_of(at, 8)
        place([cell], parts, 0)
        place([cell + 1], parts, 1)
    for i in range(4):
        place([36 + i], corner_of(RING_AT[i]), 0)
    project(16, 40)
    attend((2, 3, 4))

    projected = jnp.dot(attended[...], wout[...], preferred_element_type=F32).reshape(CELLS, 8, C)
    top, bottom = tile_row == 0, tile_row == GRID_ROWS - 1
    leftmost, rightmost = tile_col == 0, tile_col == GRID_COLS - 1
    for r in range(4):
        cells = ((36, 16, 37), (32, 0, 34), (33, 8, 35), (38, 24, 39))[r]
        picks = (slice(cells[0], cells[0] + 1), slice(cells[1], cells[1] + 8), slice(cells[2], cells[2] + 1))
        mixed = jnp.concatenate([xhi[p] + (projected[p] + bout[...]) for p in picks], axis=0).astype(BF16).astype(F32)
        col = iota((10, 8, C), 0)
        outside = (leftmost & (col == 0)) | (rightmost & (col == 9))
        if r == 0:
            outside = outside | top
        if r == 3:
            outside = outside | bottom
        mixed = jnp.where(outside, 0.0, mixed)
        for a in range(3):
            moved = sub_roll(mixed, -a) if a else mixed
            mixcat[80 * r : 80 * r + 80, a * C : (a + 1) * C] = moved.reshape(80, C).astype(BF16)

    def wait_first(i, carry):
        tap_copies(i)[0].wait()
        return carry

    lax.fori_loop(0, 27, wait_first, 0)

    def first_taps(e):
        for b in range(3):
            begin, end = ((0, 240), (0, 320), (80, 320))[b]
            t1[b, e, begin:end] = jnp.dot(mixcat[begin:end], w1[3 * b + e], preferred_element_type=F32)

    for e in range(3):
        first_taps(e)

    def t1_row(b, e, r, lanes):
        return t1[b, e, 80 * r : 80 * r + 80, lanes].reshape(10, 8, LANES)

    sum_first, sum_second = [], []
    for k in range(CHUNKS):
        lanes = slice(k * LANES, (k + 1) * LANES)
        acc, acc2 = jnp.zeros((8, LANES), F32), jnp.zeros((8, LANES), F32)
        for R in range(6):
            s = []
            for e in range(3):
                if R % 2 == 0:
                    r = R // 2
                    s.append(t1_row(0, e, r, lanes) + t1_row(1, e, r, lanes) + t1_row(2, e, r + 1, lanes))
                else:
                    r = (R + 1) // 2
                    s.append(t1_row(0, e, r - 1, lanes) + t1_row(1, e, r, lanes) + t1_row(2, e, r, lanes))
            even = s[0][0:9] + s[1][0:9] + s[2][1:10] + b1[:, lanes]
            odd = s[0][0:9] + s[1][1:10] + s[2][1:10] + b1[:, lanes]
            even = even.astype(BF16).astype(F32)
            odd = odd.astype(BF16).astype(F32)
            fs[R, 0, :, :, lanes] = even
            fs[R, 1, :, :, lanes] = odd
            if 1 <= R <= 4:
                inner_e, inner_o = even[1:9], odd[0:8]
                acc = acc + jnp.sum(inner_e, axis=0) + jnp.sum(inner_o, axis=0)
                acc2 = acc2 + jnp.sum(inner_e * inner_e, axis=0) + jnp.sum(inner_o * inner_o, axis=0)
        sum_first.append(acc)
        sum_second.append(acc2)
    packed = jnp.concatenate(
        [pack_sums(jnp.concatenate(sum_first, axis=1), 2), pack_sums(jnp.concatenate(sum_second, axis=1), 2)], axis=0
    )
    sums[1] = packed
    got2[0:2] = packed

    for kt, ks in PEERS:
        if kt == 0:
            send_sums(1, (tm, sp ^ ks), ks, got2)
        if kt == 1:
            send_sums(1, ((tm + 1) & 3, sp ^ ks), TILES + ks, got2)

    def wait_second(i, carry):
        tap_copies(i)[1].wait()
        return carry

    lax.fori_loop(0, 27, wait_second, 0)
    sums_copy(1, got2, 128).wait_recv()

    stats_own = group_stats(got2[0:64], TILES * 64 * 16)
    stats_before = group_stats(got2[64:128], TILES * 64 * 16)
    pair = []
    for which in range(2):
        rows = by_frame(stats_before[which], stats_own[which], (0, 0, 1, 1, 1, 1, 1, 1), (2, 3, 0, 1, 2, 3, 3, 3))
        rows = jnp.where(starting & (row8 < 2), jnp.broadcast_to(rows[2:3], (8, LANES)), rows)
        pair.append(spread(rows))
    mean2, scale2, bias2h = pair[0], pair[1] * (0.5 * gain2[...]), 0.5 * bias2[...]
    low4 = iota((1, 8, LANES), 1) < 4
    for R in range(6):
        for k in range(CHUNKS):
            lanes = slice(k * LANES, (k + 1) * LANES)
            both = []
            for parity in range(2):
                v = (fs[R, parity, :, :, lanes] - mean2[:, lanes]) * scale2[:, lanes] + bias2h[:, lanes]
                v = v + v * jnp.tanh(v)
                edge = 8 if parity else 0
                gone = rightmost if parity else leftmost
                if R in (0, 5):
                    missing = top if R == 0 else bottom
                    v = jnp.where(missing, 0.0, v)
                kept = jnp.where(gone, 0.0, v[edge : edge + 1])
                both.append(jnp.concatenate([v[0:8], kept] if parity else [kept, v[1:9]], axis=0))
            for a in range(3):
                joined = []
                for parity in range(2):
                    lower, upper = both[parity][0:5], both[parity][4:9]
                    lower = sub_roll(lower, -a) if a else lower
                    joined.append(jnp.where(low4, lower, sub_roll(upper, 4 - a)))
                tile = jnp.concatenate(joined, axis=1).reshape(80, LANES).astype(BF16)
                actcat[80 * R : 80 * R + 80, a * C + k * LANES : a * C + (k + 1) * LANES] = tile

    def second_taps(e):
        for b in range(3):
            begin, end = ((0, 400), (80, 400), (80, 480))[b]
            t2[b, e, begin:end] = jnp.dot(actcat[begin:end], w2[3 * b + e], preferred_element_type=F32)

    for e in range(3):
        second_taps(e)

    to, fro = iota((128, 128), 0), iota((128, 128), 1)
    place_f, place_col = to >> 5, to & 31
    j = place_col >> 1
    source = (place_col & 1) * 64 + (j & 7) * 8 + (j >> 3) * 4 + place_f
    shuffle = jnp.where(fro == source, 1.0, 0.0).astype(BF16)
    for row in range(8):
        R = row // 2 + 1
        s = []
        for e in range(3):
            picks = (R - 1, R, R) if row % 2 == 0 else (R, R, R + 1)
            terms = [t2[b, e, 80 * at : 80 * at + 80].reshape(10, 8, C2) for b, at in enumerate(picks)]
            s.append(terms[0] + terms[1] + terms[2])
        q0 = s[0][0:8] + s[1][1:9] + s[2][1:9] + b2[...]
        q1 = s[0][1:9] + s[1][1:9] + s[2][2:10] + b2[...]
        stacked = jnp.concatenate([q0.reshape(64, C2), q1.reshape(64, C2)], axis=0).astype(BF16)
        final = jnp.dot(shuffle, stacked, preferred_element_type=F32).astype(BF16)
        for f in range(FRAMES):
            out_ref[f, row] = final[32 * f : 32 * f + 32]

    block_copy(0).wait_send()
    pl.when(first_core)(lambda: ring_forward(0, 1).wait_send())
    pl.when(first_core)(lambda: centre_forward(0, 1).wait_send())

    @pl.when(tm < 2)
    def _():
        block_copy(2).wait_send()
        centre_copy(2).wait_send()

    @pl.when(tm >= 2)
    def _():
        ring_forward(2, 1).wait_send()
        centre_forward(2, 1).wait_send()

    sums_copy(0, got1, 256).wait_send()
    sums_copy(1, got2, 128).wait_send()


def per_device(
    hidden_state, norm1_gain, norm1_bias, qkv_weight, out_weight, out_bias, conv1_weight, conv1_bias,
    norm2_gain, norm2_bias, conv2_weight, conv2_bias,
):
    any_spec = pl.BlockSpec(memory_space=pl.ANY)
    decoded = pl.pallas_call(
        kernel,
        out_shape=pltpu.VMEM((FRAMES, 8, 32, C2), BF16),
        in_specs=[any_spec] * 12,
        out_specs=pl.BlockSpec(memory_space=pltpu.VMEM),
        scratch_shapes=[
            pltpu.VMEM((FRAMES, 2, 8, C), BF16),
            pltpu.VMEM((1, C), F32),
            pltpu.VMEM((1, C), F32),
            pltpu.VMEM((C, 3 * C), BF16),
            pltpu.VMEM((C, C), BF16),
            pltpu.VMEM((1, C), F32),
            pltpu.VMEM((9, 3 * C, C), BF16),
            pltpu.VMEM((1, C), F32),
            pltpu.VMEM((1, C), F32),
            pltpu.VMEM((1, C), F32),
            pltpu.VMEM((9, 3 * C, C2), BF16),
            pltpu.VMEM((1, C2), F32),
            pltpu.VMEM((128, LANES), BF16),
            pltpu.VMEM((4, BLOCK_ROWS, LANES), BF16),
            pltpu.VMEM((2, 2, LANES), F32),
            pltpu.VMEM((256, LANES), F32),
            pltpu.VMEM((128, LANES), F32),
            pltpu.VMEM((CELLS, 8, C), F32),
            pltpu.VMEM((CELLS, 16, C), BF16),
            pltpu.VMEM((CELLS * 8, C), BF16),
            pltpu.VMEM((CELLS * 16, C), BF16),
            pltpu.VMEM((CELLS * 16, C), BF16),
            pltpu.VMEM((CELLS * 8, C), BF16),
            pltpu.VMEM((CELLS * 8, 3 * C), BF16),
            pltpu.VMEM((3, 3, CELLS * 8, C), F32),
            pltpu.VMEM((6, 2, 9, 8, C), F32),
            pltpu.VMEM((480, 3 * C), BF16),
            pltpu.VMEM((3, 3, 480, C2), F32),
            pltpu.SemaphoreType.DMA((10,)),
            pltpu.SemaphoreType.DMA((27,)),
            pltpu.SemaphoreType.DMA((27,)),
            pltpu.SemaphoreType.DMA((SHARDS,)),
            pltpu.SemaphoreType.DMA((SHARDS,)),
            pltpu.SemaphoreType.DMA((2,)),
            pltpu.SemaphoreType.DMA((SHARDS,)),
            pltpu.SemaphoreType.DMA((SHARDS,)),
            pltpu.SemaphoreType.DMA((2,)),
            pltpu.SemaphoreType.DMA((2,)),
            pltpu.SemaphoreType.DMA((2,)),
        ],
        compiler_params=pltpu.CompilerParams(collective_id=0, has_side_effects=True, vmem_limit_bytes=60 << 20),
    )(
        hidden_state.reshape(FRAMES, 2, 8, C),
        norm1_gain.reshape(1, C),
        norm1_bias.reshape(1, C),
        qkv_weight,
        out_weight,
        out_bias.reshape(1, C),
        conv1_weight.reshape(27, C, C),
        conv1_bias.reshape(1, C),
        norm2_gain.reshape(1, C),
        norm2_bias.reshape(1, C),
        conv2_weight.reshape(27, C, C2),
        conv2_bias.reshape(1, C2),
    )
    return decoded[:, None]


def solution(mesh):
    return jax.shard_map(
        per_device,
        mesh=mesh,
        in_specs=(P("tm", "space", None, None, None),) + (P(),) * 11,
        out_specs=P("tm", "space", None, None, None),
        check_vma=False,
    )
```

```python
import jax
import jax.numpy as jnp
from jax import lax
from jax.experimental import pallas as pl
from jax.experimental.pallas import tpu as pltpu
from jax.sharding import PartitionSpec as P

F32, BF16 = jnp.float32, jnp.bfloat16
MESH = pl.DeviceIdType.MESH
C, C2, LANES = 512, 256, 128
CHUNKS = C // LANES
GRID_COLS, GRID_ROWS, TILES, SHARDS = 4, 8, 32, 4
FRAMES = 4
CELLS = 40

def hops(kt, ks):
    return sum((0, 1, 2, 1)[v] for v in (ks >> 3, (ks >> 1) & 3, (ks & 1) * 2 + (kt >> 1)))


PEERS = sorted(((kt, ks) for kt in range(SHARDS) for ks in range(TILES) if kt or ks), key=lambda p: -hops(*p))
EPS = 1e-6
RING = ((-1, -1), (-1, 1), (1, -1), (1, 1), (-1, 0), (1, 0), (0, -1), (0, 1))
RING_ROWS = (16, 16, 16, 16, 128, 128, 32, 32)
RING_AT = (576, 592, 608, 624, 256, 384, 512, 544)
BLOCK_ROWS = 640


def iota(shape, axis):
    return lax.broadcasted_iota(jnp.int32, shape, axis)


def lane_roll(value, shift):
    return pltpu.roll(value, shift % LANES, axis=value.ndim - 1)


def sub_roll(value, shift):
    return pltpu.roll(value, shift % 8, axis=value.ndim - 2)


def by_chunk(value, rows):
    parts = [
        value[i : i + rows, k * LANES : (k + 1) * LANES] for i in range(0, value.shape[0], rows) for k in range(CHUNKS)
    ]
    return jnp.concatenate(parts, axis=0)


def pack_sums(total, first_row):
    lane = iota((8, LANES), 1)
    row = iota((8, LANES), 0)
    merged = jnp.zeros((8, LANES), F32)
    for k in range(CHUNKS):
        part = total[:, k * LANES : (k + 1) * LANES]
        for step in (1, 2, 4, 8):
            part = part + lane_roll(part, -step)
        part = jnp.where((lane & 15) == 0, part, 0.0)
        merged = merged + (lane_roll(part, k) if k else part)
    placed = jnp.zeros((8, LANES), F32)
    for f in range(FRAMES):
        placed = placed + jnp.where(row == first_row + f, lane_roll(merged, 4 * f) if f else merged, 0.0)
    return jnp.sum(placed, axis=0, keepdims=True)


def group_stats(block, count):
    return row_stats(block_total(block), count)


def block_total(block):
    total = jnp.sum(block.reshape(8, 8, LANES), axis=0)
    total = total + sub_roll(total, 2)
    return total + sub_roll(total, 4)


def row_stats(total, count):
    mean = total[0:1] * (1.0 / count)
    square = total[1:2] * (1.0 / count)
    scale = lax.rsqrt(square - mean * mean + EPS)
    return jnp.broadcast_to(mean, (8, LANES)), jnp.broadcast_to(scale, (8, LANES))


def by_frame(first, second, second_rows, frames):
    row = iota((8, LANES), 0)
    out = jnp.zeros((8, LANES), F32)
    for f in range(FRAMES):
        moved = (lane_roll(first, -4 * f), lane_roll(second, -4 * f)) if f else (first, second)
        for r in range(8):
            if frames[r] == f:
                out = jnp.where(row == r, moved[1] if second_rows[r] else moved[0], out)
    return out


def spread(rows):
    lane = iota((8, LANES), 1)
    parts = []
    for k in range(CHUNKS):
        part = jnp.where((lane & 15) == 0, lane_roll(rows, -k) if k else rows, 0.0)
        for step in (1, 2, 4, 8):
            part = part + lane_roll(part, step)
        parts.append(part)
    return jnp.concatenate(parts, axis=1)


def kernel(
    hid_hbm, gain1_hbm, bias1_hbm, wqkv_hbm, wout_hbm, bout_hbm, w1_hbm, b1_hbm, gain2_hbm, bias2_hbm, w2_hbm, b2_hbm,
    out_ref,
    hid, gain1, bias1, wqkv, wout, bout, w1, b1, gain2, bias2, w2, b2,
    side, hbuf, sums, got1, got2, pair_out, pair_in, xhi, normed, queries, keys, wmix, attended, mixcat, t1, fs, actcat, t2,
    small_sem, w1_sem, w2_sem, hid_send, hid_recv, pass_send, cen_send, cen_recv, cpass_send, sum_send, sum_recv, pair_sem,
):
    tm = lax.axis_index("tm")
    sp = lax.axis_index("space")
    tile_row, tile_col = sp >> 2, sp & 3

    smalls = [
        pltpu.make_async_copy(a, b, small_sem.at[i])
        for i, (a, b) in enumerate(
            (
                (hid_hbm, hid), (wqkv_hbm, wqkv), (wout_hbm, wout), (gain1_hbm, gain1), (bias1_hbm, bias1),
                (bout_hbm, bout), (b1_hbm, b1), (gain2_hbm, gain2), (bias2_hbm, bias2), (b2_hbm, b2),
            )
        )
    ]
    for copy in smalls:
        copy.start()

    barrier = pltpu.get_barrier_semaphore()
    def greet(shard, tile):
        pl.semaphore_signal(barrier, inc=1, device_id=(shard, tile), device_id_type=MESH)

    for kt, ks in PEERS:
        if kt != 3:
            greet((tm + 3) & 3 if kt == 1 else tm ^ kt, sp ^ ks)
    pl.when((tm & 1) == 0)(lambda: greet(tm + 1, sp))

    def tap_copies(i):
        a, be = i // 9, lax.rem(i, 9)
        rows = pl.ds(pl.multiple_of(a * C, C), C)
        return (
            pltpu.make_async_copy(w1_hbm.at[i], w1.at[be, rows], w1_sem.at[i]),
            pltpu.make_async_copy(w2_hbm.at[i], w2.at[be, rows], w2_sem.at[i]),
        )

    def start_first(i, carry):
        tap_copies(i)[0].start()
        return carry

    def start_second(i, carry):
        tap_copies(i)[1].start()
        return carry

    lax.fori_loop(0, 27, start_first, 0)
    lax.fori_loop(0, 27, start_second, 0)

    for dt in range(1, SHARDS):
        @pl.when(tm < dt)
        def _():
            hbuf[3 - dt] = jnp.zeros((BLOCK_ROWS, LANES), BF16)

    for copy in smalls:
        copy.wait()
    order_out, order_in = iota((64, 64), 0), iota((64, 64), 1)
    wanted = (order_out & 3) * 16 + (order_out >> 2)
    permute = jnp.where(order_in == wanted, 1.0, 0.0).astype(BF16)
    plain = hid[...].astype(F32).reshape(64, C).astype(BF16)
    mine = jnp.dot(permute, plain, preferred_element_type=F32)
    hbuf[3, 0:256] = by_chunk(mine, 32).astype(BF16)
    low2 = iota((8, LANES), 0) < 4
    edges = (
        jnp.where(iota((8, C), 0) < 4, mine[0:8], sub_roll(mine[32:40], 4)),
        jnp.where(iota((8, C), 0) < 4, sub_roll(mine[24:32], 4), mine[56:64]),
    )
    for i, edge in enumerate(edges):
        side[32 * i : 32 * i + 32] = by_chunk(edge, 8).astype(BF16)
        chunk = [edge[:, k * LANES : (k + 1) * LANES] for k in range(CHUNKS)]
        upper = [jnp.where(low2, chunk[k], sub_roll(chunk[k + 1], 4)) for k in (0, 2)]
        lower = [jnp.where(low2, sub_roll(chunk[k], 4), chunk[k + 1]) for k in (0, 2)]
        side[64 + 16 * i : 80 + 16 * i] = jnp.concatenate(upper, axis=0).astype(BF16)
        side[96 + 16 * i : 112 + 16 * i] = jnp.concatenate(lower, axis=0).astype(BF16)
    pairs = mine.reshape(8, 8, C)
    first = jnp.sum(pairs, axis=0)
    second = jnp.sum(pairs * pairs, axis=0)
    first = first + sub_roll(first, 4)
    second = second + sub_roll(second, 4)
    packed = jnp.concatenate([pack_sums(first, 0), pack_sums(second, 0)], axis=0)
    sums[0] = packed
    got1[0:2] = packed

    wmix[...] = jnp.dot(wqkv[:, 2 * C :], wout[...], preferred_element_type=F32).astype(BF16)

    pl.semaphore_wait(barrier, 3 * TILES - 1 + (tm & 1))

    def send_sums(which, target, slot, buf):
        pltpu.make_async_remote_copy(
            src_ref=sums.at[which], dst_ref=buf.at[pl.ds(pl.multiple_of(slot * 2, 2), 2)],
            send_sem=sum_send.at[which], recv_sem=sum_recv.at[which], device_id=target, device_id_type=MESH,
        ).start()

    for kt, ks in PEERS:
        if kt in (0, 2):
            send_sums(0, (tm ^ kt, sp ^ ks), (kt // 2) * TILES + ks, got1)

    def piece(dr, dc):
        if dc == 0:
            return hbuf.at[3, pl.ds(0, 128)] if dr < 0 else hbuf.at[3, pl.ds(128, 128)]
        column = 0 if dc < 0 else 1
        if dr == 0:
            return side.at[pl.ds(32 * column, 32)]
        return side.at[pl.ds((64 if dr < 0 else 96) + 16 * column, 16)]

    def ring_push(dt):
        def push(src, at, rows, target):
            pltpu.make_async_remote_copy(
                src_ref=src, dst_ref=hbuf.at[3 - dt, pl.ds(at, rows)], send_sem=hid_send.at[dt],
                recv_sem=hid_recv.at[dt], device_id=target, device_id_type=MESH,
            ).start()

        for i, (dr, dc) in enumerate(RING):
            there = ((tile_row + dr) & 7) * GRID_COLS + ((tile_col + dc) & 3)
            push(piece(dr, dc), RING_AT[RING.index((-dr, -dc))], RING_ROWS[i], (tm + dt, there))

    ring_push(0)
    pl.when(tm < 2)(lambda: ring_push(2))

    RING_PART, CENTRE = pl.ds(256, 384), pl.ds(0, 256)

    def block_copy(dt):
        ref = hbuf.at[3 - dt, RING_PART]
        return pltpu.make_async_remote_copy(
            src_ref=ref, dst_ref=ref, send_sem=hid_send.at[dt], recv_sem=hid_recv.at[dt],
            device_id=(tm ^ 1, sp), device_id_type=MESH,
        )

    def centre_copy(dt):
        return pltpu.make_async_remote_copy(
            src_ref=hbuf.at[3, CENTRE], dst_ref=hbuf.at[3 - dt, CENTRE], send_sem=cen_send.at[dt],
            recv_sem=cen_recv.at[dt], device_id=(tm + dt, sp), device_id_type=MESH,
        )

    def forward(here, there, part, sends, recvs):
        return pltpu.make_async_remote_copy(
            src_ref=hbuf.at[3 - here, part], dst_ref=hbuf.at[3 - there, part], send_sem=sends.at[here // 2],
            recv_sem=recvs.at[there], device_id=(tm ^ 1, sp), device_id_type=MESH,
        )

    def ring_forward(here, there):
        return forward(here, there, RING_PART, pass_send, hid_recv)

    def centre_forward(here, there):
        return forward(here, there, CENTRE, cpass_send, cen_recv)

    def sums_copy(which, buf, rows):
        ref = buf.at[pl.ds(2, rows - 2)]
        return pltpu.make_async_remote_copy(
            src_ref=ref, dst_ref=ref, send_sem=sum_send.at[which], recv_sem=sum_recv.at[which],
            device_id=(tm ^ 1, sp), device_id_type=MESH,
        )

    def pass_on(copy_in, passing):
        @pl.when(tm >= 2)
        def _():
            copy_in(2).wait_recv()
            pl.when(first_core)(lambda: passing(2, 3).start())
            pl.when(jnp.logical_not(first_core))(lambda: passing(2, 1).start())

    def await_passed(copy_in):
        pl.when(tm >= 1)(lambda: copy_in(1).wait_recv())
        pl.when(tm == 3)(lambda: copy_in(3).wait_recv())

    first_core = (tm & 1) == 0
    pl.when(tm < 2)(lambda: centre_copy(2).start())
    pl.when(first_core)(lambda: centre_forward(0, 1).start())
    pass_on(centre_copy, centre_forward)
    await_passed(centre_copy)
    sums_copy(0, got1, 128).wait_recv()

    starting = tm == 0
    row8 = iota((8, LANES), 0)
    mine_two = jnp.where(row8 < 2, block_total(got1[0:64]), block_total(got1[64:128]))
    pair_out[...] = mine_two
    pair_copy = pltpu.make_async_remote_copy(
        src_ref=pair_out, dst_ref=pair_in, send_sem=pair_sem.at[0], recv_sem=pair_sem.at[1],
        device_id=(tm ^ 1, sp), device_id_type=MESH,
    )
    pair_copy.start()
    pair_copy.wait()
    other_two = pair_in[...]
    near, far = other_two[0:2], other_two[2:4]
    stats = [
        row_stats(total, TILES * 16 * 16)
        for total in (
            mine_two[0:2], jnp.where(first_core, far, near), mine_two[2:4], jnp.where(first_core, near, far),
        )
    ]
    span = (0, 0, 0, 0, 1, 1, 1, 1)
    steps = (0, 1, 2, 3, 0, 1, 2, 3)
    normers = []
    for half in range(2):
        pair = []
        for which in range(2):
            rows = by_frame(stats[3 - 2 * half][which], stats[2 - 2 * half][which], span, steps)
            if half:
                rows = jnp.where(starting & (row8 < 4), jnp.broadcast_to(rows[4:5], (8, LANES)), rows)
            pair.append(spread(rows))
        normers.append((pair[0], pair[1] * gain1[...]))
    shift1 = bias1[...]
    low = iota((1, 8, C), 1) < 4

    def place(cells, parts, odd):
        halves = []
        for half in range(2):
            a, b = parts[2 * half], parts[2 * half + 1]
            if odd:
                a = sub_roll(a, 4)
            else:
                b = sub_roll(b, 4)
            halves.append(jnp.where(low, a, b))
        lo, hi = halves
        hi = jnp.where(starting & low, jnp.broadcast_to(hi[:, 4:5], hi.shape), hi)
        nlo = (lo - normers[0][0]) * normers[0][1] + shift1
        nhi = (hi - normers[1][0]) * normers[1][1] + shift1
        for i, cell in enumerate(cells):
            xhi[cell] = hi[i]
            normed[cell] = jnp.concatenate([nlo[i], nhi[i]], axis=0).astype(BF16)

    def rows_of(at, rows):
        out = []
        for s in range(4):
            value = hbuf[s, at : at + CHUNKS * rows].astype(F32)
            value = jnp.concatenate([value[k * rows : (k + 1) * rows] for k in range(CHUNKS)], axis=1)
            out.append(value.reshape(rows // 8, 8, C))
        return out

    def corner_of(at):
        out = []
        for s in range(4):
            value = hbuf[s, at : at + 16].astype(F32)
            halves = (value[0:8], value[8:16])
            value = jnp.concatenate([sub_roll(halves[k // 2], 4 * (k & 1)) if k & 1 else halves[k // 2] for k in range(CHUNKS)], axis=1)
            out.append(value.reshape(1, 8, C))
        return out

    def line(at, cell):
        parts = rows_of(at, 32)
        for odd in range(2):
            place([cell + 2 * i + odd for i in range(4)], parts, odd)

    def project(begin, end):
        for g in range(begin // 2, end // 2):
            two = normed[2 * g : 2 * g + 2].astype(F32)
            queries[16 * g : 16 * g + 16] = jnp.concatenate([two[0, 8:16], two[1, 8:16]], axis=0).astype(BF16)
        asking, rows = slice(8 * begin, 8 * end), slice(16 * begin, 16 * end)
        queries[asking] = jnp.dot(queries[asking], wqkv[:, 0:C], preferred_element_type=F32).astype(BF16)
        part = normed[begin:end].reshape((end - begin) * 16, C)
        keys[rows] = jnp.dot(part, wqkv[:, C : 2 * C], preferred_element_type=F32).astype(BF16)

    q_row, k_col = iota((64, 128), 0), iota((64, 128), 1)
    first_frame = 12 - 4 * tm
    q_frame = jnp.maximum((q_row & 7) + 8, first_frame)
    k_frame = k_col & 15
    allowed = ((q_row >> 3) == (k_col >> 4)) & (k_frame <= q_frame) & (k_frame >= first_frame)

    def attend(groups):
        scores = [
            lax.dot_general(
                queries[64 * g : 64 * g + 64], keys[128 * g : 128 * g + 128], (((1,), (1,)), ((), ())),
                preferred_element_type=F32,
            )
            for g in groups
        ]
        weights, totals = [], []
        for part in scores:
            part = jnp.where(allowed, part * C ** (-0.5), -1e30)
            part = jnp.exp(part - jnp.max(part, axis=1, keepdims=True))
            part = jnp.where(allowed, part, 0.0)
            totals.append(jnp.sum(part, axis=1, keepdims=True))
            weights.append(part.astype(BF16))
        summed = [
            jnp.dot(part, normed[8 * g : 8 * g + 8].reshape(128, C), preferred_element_type=F32)
            for part, g in zip(weights, groups)
        ]
        for part, total, g in zip(summed, totals, groups):
            attended[64 * g : 64 * g + 64] = (part / total).astype(BF16)

    line(0, 0)
    line(128, 8)
    project(0, 16)
    block_copy(0).wait_recv()
    pl.when(first_core)(lambda: ring_forward(0, 1).start())
    pass_on(block_copy, ring_forward)
    attend((0, 1))
    await_passed(block_copy)
    line(256, 16)
    line(384, 24)
    for at, cell in ((512, 32), (544, 34)):
        parts = rows_of(at, 8)
        place([cell], parts, 0)
        place([cell + 1], parts, 1)
    for i in range(4):
        place([36 + i], corner_of(RING_AT[i]), 0)
    project(16, 40)
    attend((2, 3, 4))

    projected = jnp.dot(attended[...], wmix[...], preferred_element_type=F32).reshape(CELLS, 8, C)
    top, bottom = tile_row == 0, tile_row == GRID_ROWS - 1
    leftmost, rightmost = tile_col == 0, tile_col == GRID_COLS - 1
    for r in range(4):
        cells = ((36, 16, 37), (32, 0, 34), (33, 8, 35), (38, 24, 39))[r]
        picks = (slice(cells[0], cells[0] + 1), slice(cells[1], cells[1] + 8), slice(cells[2], cells[2] + 1))
        mixed = jnp.concatenate([xhi[p] + (projected[p] + bout[...]) for p in picks], axis=0).astype(BF16).astype(F32)
        col = iota((10, 8, C), 0)
        outside = (leftmost & (col == 0)) | (rightmost & (col == 9))
        if r == 0:
            outside = outside | top
        if r == 3:
            outside = outside | bottom
        mixed = jnp.where(outside, 0.0, mixed)
        for a in range(3):
            moved = sub_roll(mixed, -a) if a else mixed
            mixcat[80 * r : 80 * r + 80, a * C : (a + 1) * C] = moved.reshape(80, C).astype(BF16)

    def wait_first(i, carry):
        tap_copies(i)[0].wait()
        return carry

    lax.fori_loop(0, 27, wait_first, 0)

    def first_taps(e):
        for b in range(3):
            begin, end = ((0, 240), (0, 320), (80, 320))[b]
            t1[b, e, begin:end] = jnp.dot(mixcat[begin:end], w1[3 * b + e], preferred_element_type=F32)

    for e in range(3):
        first_taps(e)

    def t1_row(b, e, r, lanes):
        return t1[b, e, 80 * r : 80 * r + 80, lanes].reshape(10, 8, LANES)

    sum_first, sum_second = [], []
    for k in range(CHUNKS):
        lanes = slice(k * LANES, (k + 1) * LANES)
        acc, acc2 = jnp.zeros((8, LANES), F32), jnp.zeros((8, LANES), F32)
        for R in range(6):
            s = []
            for e in range(3):
                if R % 2 == 0:
                    r = R // 2
                    s.append(t1_row(0, e, r, lanes) + t1_row(1, e, r, lanes) + t1_row(2, e, r + 1, lanes))
                else:
                    r = (R + 1) // 2
                    s.append(t1_row(0, e, r - 1, lanes) + t1_row(1, e, r, lanes) + t1_row(2, e, r, lanes))
            even = s[0][0:9] + s[1][0:9] + s[2][1:10] + b1[:, lanes]
            odd = s[0][0:9] + s[1][1:10] + s[2][1:10] + b1[:, lanes]
            even = even.astype(BF16).astype(F32)
            odd = odd.astype(BF16).astype(F32)
            fs[R, 0, :, :, lanes] = even
            fs[R, 1, :, :, lanes] = odd
            if 1 <= R <= 4:
                inner_e, inner_o = even[1:9], odd[0:8]
                acc = acc + jnp.sum(inner_e, axis=0) + jnp.sum(inner_o, axis=0)
                acc2 = acc2 + jnp.sum(inner_e * inner_e, axis=0) + jnp.sum(inner_o * inner_o, axis=0)
        sum_first.append(acc)
        sum_second.append(acc2)
    packed = jnp.concatenate(
        [pack_sums(jnp.concatenate(sum_first, axis=1), 2), pack_sums(jnp.concatenate(sum_second, axis=1), 2)], axis=0
    )
    sums[1] = packed
    got2[0:2] = packed

    for kt, ks in PEERS:
        if kt == 0:
            send_sums(1, (tm, sp ^ ks), ks, got2)
        if kt == 1:
            send_sums(1, ((tm + 1) & 3, sp ^ ks), TILES + ks, got2)

    def wait_second(i, carry):
        tap_copies(i)[1].wait()
        return carry

    lax.fori_loop(0, 27, wait_second, 0)
    sums_copy(1, got2, 128).wait_recv()

    stats_own = group_stats(got2[0:64], TILES * 64 * 16)
    stats_before = group_stats(got2[64:128], TILES * 64 * 16)
    pair = []
    for which in range(2):
        rows = by_frame(stats_before[which], stats_own[which], (0, 0, 1, 1, 1, 1, 1, 1), (2, 3, 0, 1, 2, 3, 3, 3))
        rows = jnp.where(starting & (row8 < 2), jnp.broadcast_to(rows[2:3], (8, LANES)), rows)
        pair.append(spread(rows))
    mean2, scale2, bias2h = pair[0], pair[1] * (0.5 * gain2[...]), 0.5 * bias2[...]
    low4 = iota((1, 8, LANES), 1) < 4
    for R in range(6):
        for k in range(CHUNKS):
            lanes = slice(k * LANES, (k + 1) * LANES)
            both = []
            for parity in range(2):
                v = (fs[R, parity, :, :, lanes] - mean2[:, lanes]) * scale2[:, lanes] + bias2h[:, lanes]
                v = v + v * jnp.tanh(v)
                edge = 8 if parity else 0
                gone = rightmost if parity else leftmost
                if R in (0, 5):
                    missing = top if R == 0 else bottom
                    v = jnp.where(missing, 0.0, v)
                kept = jnp.where(gone, 0.0, v[edge : edge + 1])
                both.append(jnp.concatenate([v[0:8], kept] if parity else [kept, v[1:9]], axis=0))
            for a in range(3):
                joined = []
                for parity in range(2):
                    lower, upper = both[parity][0:5], both[parity][4:9]
                    lower = sub_roll(lower, -a) if a else lower
                    joined.append(jnp.where(low4, lower, sub_roll(upper, 4 - a)))
                tile = jnp.concatenate(joined, axis=1).reshape(80, LANES).astype(BF16)
                actcat[80 * R : 80 * R + 80, a * C + k * LANES : a * C + (k + 1) * LANES] = tile

    def second_taps(e):
        for b in range(3):
            begin, end = ((0, 400), (80, 400), (80, 480))[b]
            t2[b, e, begin:end] = jnp.dot(actcat[begin:end], w2[3 * b + e], preferred_element_type=F32)

    for e in range(3):
        second_taps(e)

    to, fro = iota((128, 128), 0), iota((128, 128), 1)
    place_f, place_col = to >> 5, to & 31
    j = place_col >> 1
    source = (place_col & 1) * 64 + (j & 7) * 8 + (j >> 3) * 4 + place_f
    shuffle = jnp.where(fro == source, 1.0, 0.0).astype(BF16)
    for row in range(8):
        R = row // 2 + 1
        s = []
        for e in range(3):
            picks = (R - 1, R, R) if row % 2 == 0 else (R, R, R + 1)
            terms = [t2[b, e, 80 * at : 80 * at + 80].reshape(10, 8, C2) for b, at in enumerate(picks)]
            s.append(terms[0] + terms[1] + terms[2])
        q0 = s[0][0:8] + s[1][1:9] + s[2][1:9] + b2[...]
        q1 = s[0][1:9] + s[1][1:9] + s[2][2:10] + b2[...]
        stacked = jnp.concatenate([q0.reshape(64, C2), q1.reshape(64, C2)], axis=0).astype(BF16)
        final = jnp.dot(shuffle, stacked, preferred_element_type=F32).astype(BF16)
        for f in range(FRAMES):
            out_ref[f, row] = final[32 * f : 32 * f + 32]

    block_copy(0).wait_send()
    pl.when(first_core)(lambda: ring_forward(0, 1).wait_send())
    pl.when(first_core)(lambda: centre_forward(0, 1).wait_send())

    @pl.when(tm < 2)
    def _():
        block_copy(2).wait_send()
        centre_copy(2).wait_send()

    @pl.when(tm >= 2)
    def _():
        ring_forward(2, 1).wait_send()
        centre_forward(2, 1).wait_send()

    sums_copy(0, got1, 128).wait_send()
    sums_copy(1, got2, 128).wait_send()


def per_device(
    hidden_state, norm1_gain, norm1_bias, qkv_weight, out_weight, out_bias, conv1_weight, conv1_bias,
    norm2_gain, norm2_bias, conv2_weight, conv2_bias,
):
    any_spec = pl.BlockSpec(memory_space=pl.ANY)
    decoded = pl.pallas_call(
        kernel,
        out_shape=pltpu.VMEM((FRAMES, 8, 32, C2), BF16),
        in_specs=[any_spec] * 12,
        out_specs=pl.BlockSpec(memory_space=pltpu.VMEM),
        scratch_shapes=[
            pltpu.VMEM((FRAMES, 2, 8, C), BF16),
            pltpu.VMEM((1, C), F32),
            pltpu.VMEM((1, C), F32),
            pltpu.VMEM((C, 3 * C), BF16),
            pltpu.VMEM((C, C), BF16),
            pltpu.VMEM((1, C), F32),
            pltpu.VMEM((9, 3 * C, C), BF16),
            pltpu.VMEM((1, C), F32),
            pltpu.VMEM((1, C), F32),
            pltpu.VMEM((1, C), F32),
            pltpu.VMEM((9, 3 * C, C2), BF16),
            pltpu.VMEM((1, C2), F32),
            pltpu.VMEM((128, LANES), BF16),
            pltpu.VMEM((4, BLOCK_ROWS, LANES), BF16),
            pltpu.VMEM((2, 2, LANES), F32),
            pltpu.VMEM((128, LANES), F32),
            pltpu.VMEM((128, LANES), F32),
            pltpu.VMEM((8, LANES), F32),
            pltpu.VMEM((8, LANES), F32),
            pltpu.VMEM((CELLS, 8, C), F32),
            pltpu.VMEM((CELLS, 16, C), BF16),
            pltpu.VMEM((CELLS * 8, C), BF16),
            pltpu.VMEM((CELLS * 16, C), BF16),
            pltpu.VMEM((C, C), BF16),
            pltpu.VMEM((CELLS * 8, C), BF16),
            pltpu.VMEM((CELLS * 8, 3 * C), BF16),
            pltpu.VMEM((3, 3, CELLS * 8, C), F32),
            pltpu.VMEM((6, 2, 9, 8, C), F32),
            pltpu.VMEM((480, 3 * C), BF16),
            pltpu.VMEM((3, 3, 480, C2), F32),
            pltpu.SemaphoreType.DMA((10,)),
            pltpu.SemaphoreType.DMA((27,)),
            pltpu.SemaphoreType.DMA((27,)),
            pltpu.SemaphoreType.DMA((SHARDS,)),
            pltpu.SemaphoreType.DMA((SHARDS,)),
            pltpu.SemaphoreType.DMA((2,)),
            pltpu.SemaphoreType.DMA((SHARDS,)),
            pltpu.SemaphoreType.DMA((SHARDS,)),
            pltpu.SemaphoreType.DMA((2,)),
            pltpu.SemaphoreType.DMA((2,)),
            pltpu.SemaphoreType.DMA((2,)),
            pltpu.SemaphoreType.DMA((2,)),
        ],
        compiler_params=pltpu.CompilerParams(collective_id=0, has_side_effects=True, vmem_limit_bytes=60 << 20),
    )(
        hidden_state.reshape(FRAMES, 2, 8, C),
        norm1_gain.reshape(1, C),
        norm1_bias.reshape(1, C),
        qkv_weight,
        out_weight,
        out_bias.reshape(1, C),
        conv1_weight.reshape(27, C, C),
        conv1_bias.reshape(1, C),
        norm2_gain.reshape(1, C),
        norm2_bias.reshape(1, C),
        conv2_weight.reshape(27, C, C2),
        conv2_bias.reshape(1, C2),
    )
    return decoded[:, None]


def solution(mesh):
    return jax.shard_map(
        per_device,
        mesh=mesh,
        in_specs=(P("tm", "space", None, None, None),) + (P(),) * 11,
        out_specs=P("tm", "space", None, None, None),
        check_vma=False,
    )
```

```python
import jax
import jax.numpy as jnp
from jax import lax
from jax.experimental import pallas as pl
from jax.experimental.pallas import tpu as pltpu
from jax.sharding import PartitionSpec as P

F32, BF16 = jnp.float32, jnp.bfloat16
MESH = pl.DeviceIdType.MESH
C, C2, LANES = 512, 256, 128
CHUNKS = C // LANES
GRID_COLS, GRID_ROWS, TILES, SHARDS = 4, 8, 32, 4
FRAMES = 4
CELLS = 40

def hops(kt, ks):
    return sum((0, 1, 2, 1)[v] for v in (ks >> 3, (ks >> 1) & 3, (ks & 1) * 2 + (kt >> 1)))


PEERS = sorted(((kt, ks) for kt in range(SHARDS) for ks in range(TILES) if kt or ks), key=lambda p: -hops(*p))
EPS = 1e-6
RING = ((-1, -1), (-1, 1), (1, -1), (1, 1), (-1, 0), (1, 0), (0, -1), (0, 1))
RING_ROWS = (16, 16, 16, 16, 128, 128, 32, 32)
RING_AT = (576, 592, 608, 624, 256, 384, 512, 544)
BLOCK_ROWS = 640


def iota(shape, axis):
    return lax.broadcasted_iota(jnp.int32, shape, axis)


def lane_roll(value, shift):
    return pltpu.roll(value, shift % LANES, axis=value.ndim - 1)


def sub_roll(value, shift):
    return pltpu.roll(value, shift % 8, axis=value.ndim - 2)


def by_chunk(value, rows):
    parts = [
        value[i : i + rows, k * LANES : (k + 1) * LANES] for i in range(0, value.shape[0], rows) for k in range(CHUNKS)
    ]
    return jnp.concatenate(parts, axis=0)


def pack_sums(total, first_row):
    lane = iota((8, LANES), 1)
    row = iota((8, LANES), 0)
    merged = jnp.zeros((8, LANES), F32)
    for k in range(CHUNKS):
        part = total[:, k * LANES : (k + 1) * LANES]
        for step in (1, 2, 4, 8):
            part = part + lane_roll(part, -step)
        part = jnp.where((lane & 15) == 0, part, 0.0)
        merged = merged + (lane_roll(part, k) if k else part)
    placed = jnp.zeros((8, LANES), F32)
    for f in range(FRAMES):
        placed = placed + jnp.where(row == first_row + f, lane_roll(merged, 4 * f) if f else merged, 0.0)
    return jnp.sum(placed, axis=0, keepdims=True)


def group_stats(block, count):
    total = jnp.sum(block.reshape(8, 8, LANES), axis=0)
    total = total + sub_roll(total, 2)
    total = total + sub_roll(total, 4)
    mean = total[0:1] * (1.0 / count)
    square = total[1:2] * (1.0 / count)
    scale = lax.rsqrt(square - mean * mean + EPS)
    return jnp.broadcast_to(mean, (8, LANES)), jnp.broadcast_to(scale, (8, LANES))


def by_frame(first, second, second_rows, frames):
    row = iota((8, LANES), 0)
    out = jnp.zeros((8, LANES), F32)
    for f in range(FRAMES):
        moved = (lane_roll(first, -4 * f), lane_roll(second, -4 * f)) if f else (first, second)
        for r in range(8):
            if frames[r] == f:
                out = jnp.where(row == r, moved[1] if second_rows[r] else moved[0], out)
    return out


def spread(rows):
    lane = iota((8, LANES), 1)
    parts = []
    for k in range(CHUNKS):
        part = jnp.where((lane & 15) == 0, lane_roll(rows, -k) if k else rows, 0.0)
        for step in (1, 2, 4, 8):
            part = part + lane_roll(part, step)
        parts.append(part)
    return jnp.concatenate(parts, axis=1)


def kernel(
    hid_hbm, gain1_hbm, bias1_hbm, wqkv_hbm, wout_hbm, bout_hbm, w1_hbm, b1_hbm, gain2_hbm, bias2_hbm, w2_hbm, b2_hbm,
    out_ref,
    hid, gain1, bias1, wqkv, wout, bout, w1, b1, gain2, bias2, w2, b2,
    side, hbuf, sums, got1, got2, xhi, normed, queries, keys, values, attended, mixcat, t1, fs, actcat, t2,
    small_sem, w1_sem, w2_sem, hid_send, hid_recv, pass_send, cen_send, cen_recv, cpass_send, sum_send, sum_recv,
):
    tm = lax.axis_index("tm")
    sp = lax.axis_index("space")
    tile_row, tile_col = sp >> 2, sp & 3

    smalls = [
        pltpu.make_async_copy(a, b, small_sem.at[i])
        for i, (a, b) in enumerate(
            (
                (hid_hbm, hid), (wqkv_hbm, wqkv), (wout_hbm, wout), (gain1_hbm, gain1), (bias1_hbm, bias1),
                (bout_hbm, bout), (b1_hbm, b1), (gain2_hbm, gain2), (bias2_hbm, bias2), (b2_hbm, b2),
            )
        )
    ]
    for copy in smalls:
        copy.start()

    barrier = pltpu.get_barrier_semaphore()
    for kt, ks in PEERS:
        pl.semaphore_signal(barrier, inc=1, device_id=(tm ^ kt, sp ^ ks), device_id_type=MESH)

    def tap_copies(i):
        a, be = i // 9, lax.rem(i, 9)
        rows = pl.ds(pl.multiple_of(a * C, C), C)
        return (
            pltpu.make_async_copy(w1_hbm.at[i], w1.at[be, rows], w1_sem.at[i]),
            pltpu.make_async_copy(w2_hbm.at[i], w2.at[be, rows], w2_sem.at[i]),
        )

    def start_first(i, carry):
        tap_copies(i)[0].start()
        return carry

    def start_second(i, carry):
        tap_copies(i)[1].start()
        return carry

    lax.fori_loop(0, 27, start_first, 0)
    lax.fori_loop(0, 27, start_second, 0)

    for dt in range(1, SHARDS):
        @pl.when(tm < dt)
        def _():
            hbuf[3 - dt] = jnp.zeros((BLOCK_ROWS, LANES), BF16)

    for copy in smalls:
        copy.wait()
    order_out, order_in = iota((64, 64), 0), iota((64, 64), 1)
    wanted = (order_out & 3) * 16 + (order_out >> 2)
    permute = jnp.where(order_in == wanted, 1.0, 0.0).astype(BF16)
    plain = hid[...].astype(F32).reshape(64, C).astype(BF16)
    mine = jnp.dot(permute, plain, preferred_element_type=F32)
    hbuf[3, 0:256] = by_chunk(mine, 32).astype(BF16)
    low2 = iota((8, LANES), 0) < 4
    edges = (
        jnp.where(iota((8, C), 0) < 4, mine[0:8], sub_roll(mine[32:40], 4)),
        jnp.where(iota((8, C), 0) < 4, sub_roll(mine[24:32], 4), mine[56:64]),
    )
    for i, edge in enumerate(edges):
        side[32 * i : 32 * i + 32] = by_chunk(edge, 8).astype(BF16)
        chunk = [edge[:, k * LANES : (k + 1) * LANES] for k in range(CHUNKS)]
        upper = [jnp.where(low2, chunk[k], sub_roll(chunk[k + 1], 4)) for k in (0, 2)]
        lower = [jnp.where(low2, sub_roll(chunk[k], 4), chunk[k + 1]) for k in (0, 2)]
        side[64 + 16 * i : 80 + 16 * i] = jnp.concatenate(upper, axis=0).astype(BF16)
        side[96 + 16 * i : 112 + 16 * i] = jnp.concatenate(lower, axis=0).astype(BF16)
    pairs = mine.reshape(8, 8, C)
    first = jnp.sum(pairs, axis=0)
    second = jnp.sum(pairs * pairs, axis=0)
    first = first + sub_roll(first, 4)
    second = second + sub_roll(second, 4)
    packed = jnp.concatenate([pack_sums(first, 0), pack_sums(second, 0)], axis=0)
    sums[0] = packed
    got1[0:2] = packed

    pl.semaphore_wait(barrier, SHARDS * TILES - 1)

    def send_sums(which, target, slot, buf):
        pltpu.make_async_remote_copy(
            src_ref=sums.at[which], dst_ref=buf.at[pl.ds(pl.multiple_of(slot * 2, 2), 2)],
            send_sem=sum_send.at[which], recv_sem=sum_recv.at[which], device_id=target, device_id_type=MESH,
        ).start()

    for kt, ks in PEERS:
        send_sums(0, (tm ^ kt, sp ^ ks), kt * TILES + ks, got1)

    def piece(dr, dc):
        if dc == 0:
            return hbuf.at[3, pl.ds(0, 128)] if dr < 0 else hbuf.at[3, pl.ds(128, 128)]
        column = 0 if dc < 0 else 1
        if dr == 0:
            return side.at[pl.ds(32 * column, 32)]
        return side.at[pl.ds((64 if dr < 0 else 96) + 16 * column, 16)]

    def ring_push(dt):
        def push(src, at, rows, target):
            pltpu.make_async_remote_copy(
                src_ref=src, dst_ref=hbuf.at[3 - dt, pl.ds(at, rows)], send_sem=hid_send.at[dt],
                recv_sem=hid_recv.at[dt], device_id=target, device_id_type=MESH,
            ).start()

        for i, (dr, dc) in enumerate(RING):
            there = ((tile_row + dr) & 7) * GRID_COLS + ((tile_col + dc) & 3)
            push(piece(dr, dc), RING_AT[RING.index((-dr, -dc))], RING_ROWS[i], (tm + dt, there))

    ring_push(0)
    pl.when(tm < 2)(lambda: ring_push(2))

    RING_PART, CENTRE = pl.ds(256, 384), pl.ds(0, 256)

    def block_copy(dt):
        ref = hbuf.at[3 - dt, RING_PART]
        return pltpu.make_async_remote_copy(
            src_ref=ref, dst_ref=ref, send_sem=hid_send.at[dt], recv_sem=hid_recv.at[dt],
            device_id=(tm ^ 1, sp), device_id_type=MESH,
        )

    def centre_copy(dt):
        return pltpu.make_async_remote_copy(
            src_ref=hbuf.at[3, CENTRE], dst_ref=hbuf.at[3 - dt, CENTRE], send_sem=cen_send.at[dt],
            recv_sem=cen_recv.at[dt], device_id=(tm + dt, sp), device_id_type=MESH,
        )

    def forward(here, there, part, sends, recvs):
        return pltpu.make_async_remote_copy(
            src_ref=hbuf.at[3 - here, part], dst_ref=hbuf.at[3 - there, part], send_sem=sends.at[here // 2],
            recv_sem=recvs.at[there], device_id=(tm ^ 1, sp), device_id_type=MESH,
        )

    def ring_forward(here, there):
        return forward(here, there, RING_PART, pass_send, hid_recv)

    def centre_forward(here, there):
        return forward(here, there, CENTRE, cpass_send, cen_recv)

    def sums_copy(which, buf, rows):
        ref = buf.at[pl.ds(2, rows - 2)]
        return pltpu.make_async_remote_copy(
            src_ref=ref, dst_ref=ref, send_sem=sum_send.at[which], recv_sem=sum_recv.at[which],
            device_id=(tm ^ 1, sp), device_id_type=MESH,
        )

    def pass_on(copy_in, passing):
        @pl.when(tm >= 2)
        def _():
            copy_in(2).wait_recv()
            pl.when(first_core)(lambda: passing(2, 3).start())
            pl.when(jnp.logical_not(first_core))(lambda: passing(2, 1).start())

    def await_passed(copy_in):
        pl.when(tm >= 1)(lambda: copy_in(1).wait_recv())
        pl.when(tm == 3)(lambda: copy_in(3).wait_recv())

    first_core = (tm & 1) == 0
    pl.when(tm < 2)(lambda: centre_copy(2).start())
    pl.when(first_core)(lambda: centre_forward(0, 1).start())
    pass_on(centre_copy, centre_forward)
    await_passed(centre_copy)
    sums_copy(0, got1, 256).wait_recv()

    starting = tm == 0
    row8 = iota((8, LANES), 0)
    stats = []
    for dt in range(SHARDS):
        kt = tm ^ ((tm - dt) & 3)
        stats.append(group_stats(got1[pl.ds(pl.multiple_of(kt * 64, 64), 64)], TILES * 16 * 16))
    span = (0, 0, 0, 0, 1, 1, 1, 1)
    steps = (0, 1, 2, 3, 0, 1, 2, 3)
    normers = []
    for half in range(2):
        pair = []
        for which in range(2):
            rows = by_frame(stats[3 - 2 * half][which], stats[2 - 2 * half][which], span, steps)
            if half:
                rows = jnp.where(starting & (row8 < 4), jnp.broadcast_to(rows[4:5], (8, LANES)), rows)
            pair.append(spread(rows))
        normers.append((pair[0], pair[1] * gain1[...]))
    shift1 = bias1[...]
    low = iota((1, 8, C), 1) < 4

    def place(cells, parts, odd):
        halves = []
        for half in range(2):
            a, b = parts[2 * half], parts[2 * half + 1]
            if odd:
                a = sub_roll(a, 4)
            else:
                b = sub_roll(b, 4)
            halves.append(jnp.where(low, a, b))
        lo, hi = halves
        hi = jnp.where(starting & low, jnp.broadcast_to(hi[:, 4:5], hi.shape), hi)
        nlo = (lo - normers[0][0]) * normers[0][1] + shift1
        nhi = (hi - normers[1][0]) * normers[1][1] + shift1
        for i, cell in enumerate(cells):
            xhi[cell] = hi[i]
            normed[cell] = jnp.concatenate([nlo[i], nhi[i]], axis=0).astype(BF16)

    def rows_of(at, rows):
        out = []
        for s in range(4):
            value = hbuf[s, at : at + CHUNKS * rows].astype(F32)
            value = jnp.concatenate([value[k * rows : (k + 1) * rows] for k in range(CHUNKS)], axis=1)
            out.append(value.reshape(rows // 8, 8, C))
        return out

    def corner_of(at):
        out = []
        for s in range(4):
            value = hbuf[s, at : at + 16].astype(F32)
            halves = (value[0:8], value[8:16])
            value = jnp.concatenate([sub_roll(halves[k // 2], 4 * (k & 1)) if k & 1 else halves[k // 2] for k in range(CHUNKS)], axis=1)
            out.append(value.reshape(1, 8, C))
        return out

    def line(at, cell):
        parts = rows_of(at, 32)
        for odd in range(2):
            place([cell + 2 * i + odd for i in range(4)], parts, odd)

    def project(begin, end):
        for g in range(begin // 2, end // 2):
            two = normed[2 * g : 2 * g + 2].astype(F32)
            queries[16 * g : 16 * g + 16] = jnp.concatenate([two[0, 8:16], two[1, 8:16]], axis=0).astype(BF16)
        asking, rows = slice(8 * begin, 8 * end), slice(16 * begin, 16 * end)
        queries[asking] = jnp.dot(queries[asking], wqkv[:, 0:C], preferred_element_type=F32).astype(BF16)
        part = normed[begin:end].reshape((end - begin) * 16, C)
        keys[rows] = jnp.dot(part, wqkv[:, C : 2 * C], preferred_element_type=F32).astype(BF16)
        values[rows] = jnp.dot(part, wqkv[:, 2 * C :], preferred_element_type=F32).astype(BF16)

    q_row, k_col = iota((64, 128), 0), iota((64, 128), 1)
    first_frame = 12 - 4 * tm
    q_frame = jnp.maximum((q_row & 7) + 8, first_frame)
    k_frame = k_col & 15
    allowed = ((q_row >> 3) == (k_col >> 4)) & (k_frame <= q_frame) & (k_frame >= first_frame)

    def attend(groups):
        scores = [
            lax.dot_general(
                queries[64 * g : 64 * g + 64], keys[128 * g : 128 * g + 128], (((1,), (1,)), ((), ())),
                preferred_element_type=F32,
            )
            for g in groups
        ]
        weights, totals = [], []
        for part in scores:
            part = jnp.where(allowed, part * C ** (-0.5), -1e30)
            part = jnp.exp(part - jnp.max(part, axis=1, keepdims=True))
            part = jnp.where(allowed, part, 0.0)
            totals.append(jnp.sum(part, axis=1, keepdims=True))
            weights.append(part.astype(BF16))
        summed = [
            jnp.dot(part, values[128 * g : 128 * g + 128], preferred_element_type=F32) for part, g in zip(weights, groups)
        ]
        for part, total, g in zip(summed, totals, groups):
            attended[64 * g : 64 * g + 64] = (part / total).astype(BF16)

    line(0, 0)
    line(128, 8)
    project(0, 16)
    block_copy(0).wait_recv()
    pl.when(first_core)(lambda: ring_forward(0, 1).start())
    pass_on(block_copy, ring_forward)
    attend((0, 1))
    await_passed(block_copy)
    line(256, 16)
    line(384, 24)
    for at, cell in ((512, 32), (544, 34)):
        parts = rows_of(at, 8)
        place([cell], parts, 0)
        place([cell + 1], parts, 1)
    for i in range(4):
        place([36 + i], corner_of(RING_AT[i]), 0)
    project(16, 40)
    attend((2, 3, 4))

    projected = jnp.dot(attended[...], wout[...], preferred_element_type=F32).reshape(CELLS, 8, C)
    top, bottom = tile_row == 0, tile_row == GRID_ROWS - 1
    leftmost, rightmost = tile_col == 0, tile_col == GRID_COLS - 1
    for r in range(4):
        cells = ((36, 16, 37), (32, 0, 34), (33, 8, 35), (38, 24, 39))[r]
        picks = (slice(cells[0], cells[0] + 1), slice(cells[1], cells[1] + 8), slice(cells[2], cells[2] + 1))
        mixed = jnp.concatenate([xhi[p] + (projected[p] + bout[...]) for p in picks], axis=0).astype(BF16).astype(F32)
        col = iota((10, 8, C), 0)
        outside = (leftmost & (col == 0)) | (rightmost & (col == 9))
        if r == 0:
            outside = outside | top
        if r == 3:
            outside = outside | bottom
        mixed = jnp.where(outside, 0.0, mixed)
        for a in range(3):
            moved = sub_roll(mixed, -a) if a else mixed
            mixcat[80 * r : 80 * r + 80, a * C : (a + 1) * C] = moved.reshape(80, C).astype(BF16)

    def wait_first(i, carry):
        tap_copies(i)[0].wait()
        return carry

    lax.fori_loop(0, 27, wait_first, 0)

    def t1_row(b, e, r, lanes):
        return t1[b, e, 80 * r : 80 * r + 80, lanes].reshape(10, 8, LANES)

    sum_first, sum_second = [], []
    def gather_chunk(k):
        lanes = slice(k * LANES, (k + 1) * LANES)
        acc, acc2 = jnp.zeros((8, LANES), F32), jnp.zeros((8, LANES), F32)
        for R in range(6):
            s = []
            for e in range(3):
                if R % 2 == 0:
                    r = R // 2
                    s.append(t1_row(0, e, r, lanes) + t1_row(1, e, r, lanes) + t1_row(2, e, r + 1, lanes))
                else:
                    r = (R + 1) // 2
                    s.append(t1_row(0, e, r - 1, lanes) + t1_row(1, e, r, lanes) + t1_row(2, e, r, lanes))
            even = s[0][0:9] + s[1][0:9] + s[2][1:10] + b1[:, lanes]
            odd = s[0][0:9] + s[1][1:10] + s[2][1:10] + b1[:, lanes]
            even = even.astype(BF16).astype(F32)
            odd = odd.astype(BF16).astype(F32)
            fs[R, 0, :, :, lanes] = even
            fs[R, 1, :, :, lanes] = odd
            if 1 <= R <= 4:
                inner_e, inner_o = even[1:9], odd[0:8]
                acc = acc + jnp.sum(inner_e, axis=0) + jnp.sum(inner_o, axis=0)
                acc2 = acc2 + jnp.sum(inner_e * inner_e, axis=0) + jnp.sum(inner_o * inner_o, axis=0)
        sum_first.append(acc)
        sum_second.append(acc2)

    for n in range(2):
        cols = slice(256 * n, 256 * n + 256)
        for e in range(3):
            for b in range(3):
                begin, end = ((0, 240), (0, 320), (80, 320))[b]
                t1[b, e, begin:end, cols] = jnp.dot(
                    mixcat[begin:end], w1[3 * b + e, :, cols], preferred_element_type=F32
                )
        for k in range(2 * n, 2 * n + 2):
            gather_chunk(k)

    packed = jnp.concatenate(
        [pack_sums(jnp.concatenate(sum_first, axis=1), 2), pack_sums(jnp.concatenate(sum_second, axis=1), 2)], axis=0
    )
    sums[1] = packed
    got2[0:2] = packed

    for kt, ks in PEERS:
        if kt == 0:
            send_sums(1, (tm, sp ^ ks), ks, got2)
        if kt == 1:
            send_sums(1, ((tm + 1) & 3, sp ^ ks), TILES + ks, got2)

    def wait_second(i, carry):
        tap_copies(i)[1].wait()
        return carry

    lax.fori_loop(0, 27, wait_second, 0)
    sums_copy(1, got2, 128).wait_recv()

    stats_own = group_stats(got2[0:64], TILES * 64 * 16)
    stats_before = group_stats(got2[64:128], TILES * 64 * 16)
    pair = []
    for which in range(2):
        rows = by_frame(stats_before[which], stats_own[which], (0, 0, 1, 1, 1, 1, 1, 1), (2, 3, 0, 1, 2, 3, 3, 3))
        rows = jnp.where(starting & (row8 < 2), jnp.broadcast_to(rows[2:3], (8, LANES)), rows)
        pair.append(spread(rows))
    mean2, scale2, bias2h = pair[0], pair[1] * (0.5 * gain2[...]), 0.5 * bias2[...]
    low4 = iota((1, 8, LANES), 1) < 4
    for R in range(6):
        for k in range(CHUNKS):
            lanes = slice(k * LANES, (k + 1) * LANES)
            both = []
            for parity in range(2):
                v = (fs[R, parity, :, :, lanes] - mean2[:, lanes]) * scale2[:, lanes] + bias2h[:, lanes]
                v = v + v * jnp.tanh(v)
                edge = 8 if parity else 0
                gone = rightmost if parity else leftmost
                if R in (0, 5):
                    missing = top if R == 0 else bottom
                    v = jnp.where(missing, 0.0, v)
                kept = jnp.where(gone, 0.0, v[edge : edge + 1])
                both.append(jnp.concatenate([v[0:8], kept] if parity else [kept, v[1:9]], axis=0))
            for a in range(3):
                joined = []
                for parity in range(2):
                    lower, upper = both[parity][0:5], both[parity][4:9]
                    lower = sub_roll(lower, -a) if a else lower
                    joined.append(jnp.where(low4, lower, sub_roll(upper, 4 - a)))
                tile = jnp.concatenate(joined, axis=1).reshape(80, LANES).astype(BF16)
                actcat[80 * R : 80 * R + 80, a * C + k * LANES : a * C + (k + 1) * LANES] = tile

    def second_taps(e):
        for b in range(3):
            begin, end = ((0, 400), (80, 400), (80, 480))[b]
            t2[b, e, begin:end] = jnp.dot(actcat[begin:end], w2[3 * b + e], preferred_element_type=F32)

    for e in range(3):
        second_taps(e)

    to, fro = iota((128, 128), 0), iota((128, 128), 1)
    place_f, place_col = to >> 5, to & 31
    j = place_col >> 1
    source = (place_col & 1) * 64 + (j & 7) * 8 + (j >> 3) * 4 + place_f
    shuffle = jnp.where(fro == source, 1.0, 0.0).astype(BF16)
    for row in range(8):
        R = row // 2 + 1
        s = []
        for e in range(3):
            picks = (R - 1, R, R) if row % 2 == 0 else (R, R, R + 1)
            terms = [t2[b, e, 80 * at : 80 * at + 80].reshape(10, 8, C2) for b, at in enumerate(picks)]
            s.append(terms[0] + terms[1] + terms[2])
        q0 = s[0][0:8] + s[1][1:9] + s[2][1:9] + b2[...]
        q1 = s[0][1:9] + s[1][1:9] + s[2][2:10] + b2[...]
        stacked = jnp.concatenate([q0.reshape(64, C2), q1.reshape(64, C2)], axis=0).astype(BF16)
        final = jnp.dot(shuffle, stacked, preferred_element_type=F32).astype(BF16)
        for f in range(FRAMES):
            out_ref[f, row] = final[32 * f : 32 * f + 32]

    block_copy(0).wait_send()
    pl.when(first_core)(lambda: ring_forward(0, 1).wait_send())
    pl.when(first_core)(lambda: centre_forward(0, 1).wait_send())

    @pl.when(tm < 2)
    def _():
        block_copy(2).wait_send()
        centre_copy(2).wait_send()

    @pl.when(tm >= 2)
    def _():
        ring_forward(2, 1).wait_send()
        centre_forward(2, 1).wait_send()

    sums_copy(0, got1, 256).wait_send()
    sums_copy(1, got2, 128).wait_send()


def per_device(
    hidden_state, norm1_gain, norm1_bias, qkv_weight, out_weight, out_bias, conv1_weight, conv1_bias,
    norm2_gain, norm2_bias, conv2_weight, conv2_bias,
):
    any_spec = pl.BlockSpec(memory_space=pl.ANY)
    decoded = pl.pallas_call(
        kernel,
        out_shape=pltpu.VMEM((FRAMES, 8, 32, C2), BF16),
        in_specs=[any_spec] * 12,
        out_specs=pl.BlockSpec(memory_space=pltpu.VMEM),
        scratch_shapes=[
            pltpu.VMEM((FRAMES, 2, 8, C), BF16),
            pltpu.VMEM((1, C), F32),
            pltpu.VMEM((1, C), F32),
            pltpu.VMEM((C, 3 * C), BF16),
            pltpu.VMEM((C, C), BF16),
            pltpu.VMEM((1, C), F32),
            pltpu.VMEM((9, 3 * C, C), BF16),
            pltpu.VMEM((1, C), F32),
            pltpu.VMEM((1, C), F32),
            pltpu.VMEM((1, C), F32),
            pltpu.VMEM((9, 3 * C, C2), BF16),
            pltpu.VMEM((1, C2), F32),
            pltpu.VMEM((128, LANES), BF16),
            pltpu.VMEM((4, BLOCK_ROWS, LANES), BF16),
            pltpu.VMEM((2, 2, LANES), F32),
            pltpu.VMEM((256, LANES), F32),
            pltpu.VMEM((128, LANES), F32),
            pltpu.VMEM((CELLS, 8, C), F32),
            pltpu.VMEM((CELLS, 16, C), BF16),
            pltpu.VMEM((CELLS * 8, C), BF16),
            pltpu.VMEM((CELLS * 16, C), BF16),
            pltpu.VMEM((CELLS * 16, C), BF16),
            pltpu.VMEM((CELLS * 8, C), BF16),
            pltpu.VMEM((CELLS * 8, 3 * C), BF16),
            pltpu.VMEM((3, 3, CELLS * 8, C), F32),
            pltpu.VMEM((6, 2, 9, 8, C), F32),
            pltpu.VMEM((480, 3 * C), BF16),
            pltpu.VMEM((3, 3, 480, C2), F32),
            pltpu.SemaphoreType.DMA((10,)),
            pltpu.SemaphoreType.DMA((27,)),
            pltpu.SemaphoreType.DMA((27,)),
            pltpu.SemaphoreType.DMA((SHARDS,)),
            pltpu.SemaphoreType.DMA((SHARDS,)),
            pltpu.SemaphoreType.DMA((2,)),
            pltpu.SemaphoreType.DMA((SHARDS,)),
            pltpu.SemaphoreType.DMA((SHARDS,)),
            pltpu.SemaphoreType.DMA((2,)),
            pltpu.SemaphoreType.DMA((2,)),
            pltpu.SemaphoreType.DMA((2,)),
        ],
        compiler_params=pltpu.CompilerParams(collective_id=0, has_side_effects=True, vmem_limit_bytes=60 << 20),
    )(
        hidden_state.reshape(FRAMES, 2, 8, C),
        norm1_gain.reshape(1, C),
        norm1_bias.reshape(1, C),
        qkv_weight,
        out_weight,
        out_bias.reshape(1, C),
        conv1_weight.reshape(27, C, C),
        conv1_bias.reshape(1, C),
        norm2_gain.reshape(1, C),
        norm2_bias.reshape(1, C),
        conv2_weight.reshape(27, C, C2),
        conv2_bias.reshape(1, C2),
    )
    return decoded[:, None]


def solution(mesh):
    return jax.shard_map(
        per_device,
        mesh=mesh,
        in_specs=(P("tm", "space", None, None, None),) + (P(),) * 11,
        out_specs=P("tm", "space", None, None, None),
        check_vma=False,
    )
```
